32 devices in a mesh: blk: 8 (over y, x, core), rep: 4 (over z).
Axes of the slice: x: 2, y: 2, z: 4, core: 2. Of those that a mesh axis runs over, the one named last changes fastest.
Arguments:
- features: bfloat16 [8192, 128], P(('blk', 'rep')), may hold values from -6 to 6
- edge_rows: int32 [8, 8, 8, 512], P('blk', None, 'rep'), may hold values from 0 to 1023
- edge_cols: int32 [8, 8, 8, 512], P('blk', None, 'rep'), may hold values from 0 to 127
- weight: bfloat16 [128, 256], replicated, may hold values from -0.5 to 0.5
- bias: float32 [256], replicated, may hold values from -3 to 3
- upstream: bfloat16 [8192, 256], P('blk'), may hold values from -6 to 6
- train_mask: int32 [8192], P('blk'), may hold values 0 or 1
Outputs:
- activations: bfloat16 [8192, 256], P(('blk', 'rep'))
- grad_features: bfloat16 [8192, 128], P(('blk', 'rep'))
- grad_weight: float32 [128, 256], replicated
- grad_bias: float32 [256], replicated
The draws below stay inside these ranges and needn't reach their ends.
Inputs may be any that keep to these rules, and one draw needn't show every extreme that they name: `edge_rows`: target indices within a panel. `edge_cols`: source indices within a column block.
All inputs are finite; a program needn't handle non-finite values. No bound on the sum of `train_mask` on one device may be relied on, other than what follows from the above.
Results may differ from the reference program's by a relative error of at most 0.018.
Values may be sent and summed in bfloat16 or wider, within the bound.
A program may use at most 64 MiB of HBM per device.

```python
import jax
import jax.numpy as jnp
from jax import lax

D_IN = 128
HID = 256
CB = 128
PIECE = 256
PANEL = 1024
NODES = 8192
BLOCKS = 8
EDGES = 512
N_BLK = 8
N_REP = 4


def touch_ends(drawn, rng, least, high):
    spot = [jax.random.randint(jax.random.fold_in(rng, axis), (), 0, length) for axis, length in enumerate(drawn.shape)]
    widest = drawn.shape.index(max(drawn.shape))
    neighbour = spot[:widest] + [(spot[widest] + 1) % drawn.shape[widest]] + spot[widest + 1:]
    return drawn.at[tuple(spot)].set(least).at[tuple(neighbour)].set(high)


def level_of(rng, dims, pieces, smallest, high):
    gain = 1.0
    for dim, shards_of in pieces:
        draws = jax.random.uniform(jax.random.fold_in(jax.random.fold_in(rng, 6), dim), (shards_of,), jnp.float32, smallest / len(pieces), high / len(pieces))
        gain = gain * jnp.repeat(jnp.exp(draws), dims[dim] // shards_of).reshape((-1,) + (1,) * (len(dims) - 1 - dim))
    return gain


def noise(rng, shape, width, limit, pieces=(), held_as=jnp.bfloat16):
    drawn = jax.random.normal(rng, shape, jnp.float32) * width
    if len(pieces) > 0:
        drawn = level_of(rng, shape, pieces, -0.22, 0.18) * drawn
    return jnp.clip(drawn, min=-limit, max=limit).astype(held_as)


def setup_inputs(seed: int = 0) -> dict:
    arg_keys = jax.random.split(jax.random.key(seed), 8)
    features = noise(arg_keys[0], (NODES, D_IN), 1.0, 6.0, ((0, 32),))
    edge_rows = touch_ends(jax.random.randint(arg_keys[1], (N_BLK, N_BLK, BLOCKS, EDGES), 0, PANEL), jax.random.fold_in(arg_keys[1], 1), 0, PANEL - 1).astype(jnp.int32)
    edge_cols = touch_ends(jax.random.randint(arg_keys[2], (N_BLK, N_BLK, BLOCKS, EDGES), 0, CB), jax.random.fold_in(arg_keys[2], 1), 0, CB - 1).astype(jnp.int32)
    weight = noise(arg_keys[3], (D_IN, HID), D_IN ** -0.5, 0.5)
    bias = noise(arg_keys[4], (HID,), 0.5, 3.0, (), jnp.float32)
    upstream = noise(arg_keys[5], (NODES, HID), 1.0, 6.0, ((0, 8),))
    train_mask = touch_ends((jax.random.randint(arg_keys[6], (NODES,), 0, 4) < 1).astype(jnp.int32), jax.random.fold_in(arg_keys[6], 1), 0, 1)
    return dict(features=features, edge_rows=edge_rows, edge_cols=edge_cols, weight=weight, bias=bias, upstream=upstream, train_mask=train_mask)


def reference(features, edge_rows, edge_cols, weight, bias, upstream, train_mask):
    npanel = PIECE * N_REP
    nodes = npanel * N_BLK
    group_size = PIECE // CB
    col_base = (jnp.arange(N_BLK, dtype=jnp.int32)[:, None, None] * npanel
                + jnp.arange(npanel // CB, dtype=jnp.int32)[None, :, None] * CB)
    group_of = (jnp.arange(npanel // CB, dtype=jnp.int32) // group_size)[None, :, None]
    feats = features.astype(jnp.float32)

    def panel_sum(panel):
        targets = edge_rows[panel]
        columns = edge_cols[panel]
        sources = (col_base + columns).reshape(-1)
        segment = (group_of * npanel + targets).reshape(-1)
        values = feats[sources]
        parts = jax.ops.segment_sum(values, segment, num_segments=N_REP * npanel)
        parts = parts.reshape(N_REP, npanel, D_IN)
        parts = lax.optimization_barrier(parts.astype(jnp.bfloat16)).astype(jnp.float32)
        counts = jax.ops.segment_sum(jnp.ones((targets.size,), jnp.float32), targets.reshape(-1), num_segments=npanel)
        return jnp.sum(parts, axis=0), counts

    gathered, counts = lax.map(panel_sum, jnp.arange(N_BLK, dtype=jnp.int32))
    gathered = gathered.reshape(nodes, D_IN)
    degree = 1.0 + counts.reshape(nodes)
    mixed_in = ((feats + gathered) / degree[:, None]).astype(jnp.bfloat16)
    pre_act = jnp.dot(mixed_in, weight, preferred_element_type=jnp.float32) + bias
    gate_value = jax.nn.sigmoid(pre_act)
    activations = (pre_act * gate_value).astype(jnp.bfloat16)
    slope = gate_value * (1.0 + pre_act * (1.0 - gate_value))
    grad_pre = (upstream.astype(jnp.float32) * train_mask.astype(jnp.float32)[:, None] * slope).astype(jnp.bfloat16)
    grad_weight = lax.dot_general(mixed_in, grad_pre, (((0,), (0,)), ((), ())), preferred_element_type=jnp.float32)
    grad_bias = jnp.sum(grad_pre.astype(jnp.float32), axis=0)
    scaled_back = (jnp.dot(grad_pre, weight.T, preferred_element_type=jnp.float32) / degree[:, None]).astype(jnp.bfloat16)

    def scatter_back(running, panel):
        targets = edge_rows[panel]
        columns = edge_cols[panel]
        sources = (col_base + columns).reshape(-1)
        own_back = lax.dynamic_slice_in_dim(scaled_back, panel * npanel, npanel, 0)
        values = own_back[targets.reshape(-1)].astype(jnp.float32)
        return running + jax.ops.segment_sum(values, sources, num_segments=nodes), None

    received, _ = lax.scan(scatter_back, jnp.zeros((nodes, D_IN), jnp.float32), jnp.arange(N_BLK, dtype=jnp.int32))
    grad_features = (scaled_back.astype(jnp.float32) + received).astype(jnp.bfloat16)
    return activations, grad_features, grad_weight, grad_bias
```

```python
import functools

import jax
import jax.numpy as jnp
from jax import lax
from jax.experimental import pallas as pl
from jax.experimental.pallas import tpu as pltpu
from jax.sharding import PartitionSpec as P

CB = 128
F32 = jnp.float32
BF16 = jnp.bfloat16
MESH = pl.DeviceIdType.MESH
NT = (((1,), (1,)), ((), ()))


def column(row):
    return jnp.broadcast_to(row, (CB, CB)).T


def one_hot(index, count):
    length = index.shape[-1]
    spot = lax.broadcasted_iota(jnp.int32, (count, length), 0)
    return jnp.where(spot == index, 1.0, 0.0).astype(BF16)


def kernel(
    n_blk, n_rep, keep,
    feat_ref, rows_ref, cols_ref, weight_ref, bias_ref, mask_ref, up_hbm,
    act_ref, gf_ref, gw_ref, gb_ref,
    fbuf, amat, acc, psend, precv, upbuf, backs, oacc, gsend, grecv,
    w1s, w1r, w2s, w2r, w3s, w3r,
    f_ss, f_rs, p_ss, p_rs, b_ss, b_rs, g_ss, g_rs, w1_ss, w1_rs, w2_ss, w2_rs, w3_ss, w3_rs, up_sem,
):
    b = lax.axis_index("blk")
    z = lax.axis_index("rep")
    piece, d_in = feat_ref.shape
    panel = piece * n_rep
    hid = weight_ref.shape[1]
    chunks = piece // CB
    wch = d_in // n_blk

    def blk_at(k):
        return lax.rem(b + k, n_blk)

    def rep_at(j):
        return lax.rem(z + j, n_rep)

    def send(src, dst, ss, rs, i, **where):
        copy = pltpu.make_async_remote_copy(
            src_ref=src, dst_ref=dst, send_sem=ss.at[i], recv_sem=rs.at[i],
            device_id=where, device_id_type=MESH,
        )
        copy.start()
        return copy

    barrier = pltpu.get_barrier_semaphore()
    for k in range(1, n_blk):
        pl.semaphore_signal(barrier, inc=1, device_id={"blk": blk_at(k)}, device_id_type=MESH)
    for j in range(1, n_rep):
        pl.semaphore_signal(barrier, inc=1, device_id={"rep": rep_at(j)}, device_id_type=MESH)
    up_copy = pltpu.make_async_copy(
        up_hbm.at[pl.ds(pl.multiple_of(z * piece, piece), piece)], upbuf, up_sem
    )
    up_copy.start()
    fbuf[b] = feat_ref[...]
    pl.semaphore_wait(barrier, n_blk + n_rep - 2)

    sent = []
    f_copies = [
        send(feat_ref, fbuf.at[b], f_ss, f_rs, k, blk=blk_at(k)) for k in range(1, n_blk)
    ]
    sent += f_copies

    def build(q, slot):
        for c in range(chunks):
            rows = rows_ref[0, q, pl.ds(c, 1), :]
            cols = cols_ref[0, q, pl.ds(c, 1), :]
            length = rows.shape[-1]
            col_hot = one_hot(cols, CB)
            low_hot = one_hot(rows & (CB - 1), CB)
            high = jnp.broadcast_to(rows >> 7, (16, length))
            parts = []
            for h in range(panel // CB):
                picked = jnp.where(high == h, 1.0, 0.0).astype(BF16)
                parts.append(low_hot * jnp.concatenate([picked] * (CB // 16), axis=0))
            row_hot = jnp.concatenate(parts, axis=0)
            amat[slot, :, c * CB:(c + 1) * CB] = lax.dot_general(
                row_hot, col_hot, NT, preferred_element_type=F32
            ).astype(BF16)

    def with_ones(q):
        return jnp.concatenate([fbuf[q], jnp.ones((piece, CB), BF16)], axis=1)

    def pack(total, slot):
        psend[slot, 0:piece, :] = total[:, :d_in].astype(BF16)
        counts = total[:, d_in:]
        tall = jnp.concatenate(
            [counts[i * CB:(i + 1) * CB].T[0:16] for i in range(chunks)], axis=0
        )
        top = tall.astype(BF16).astype(F32)
        line = lax.broadcasted_iota(jnp.int32, tall.shape, 0)
        psend[slot, piece:, :] = jnp.where(line % 16 < 8, top, tall - top).astype(BF16)

    if keep:
        def build_step(q, carry):
            build(q, q)
            return carry
        lax.fori_loop(0, n_blk, build_step, 0)
        for copy in f_copies:
            copy.wait_recv()
    else:
        for copy in f_copies:
            copy.wait_recv()
        acc[...] = jnp.zeros_like(acc)

        def both_step(q, carry):
            build(q, 0)
            acc[...] += jnp.dot(amat[0], with_ones(q), preferred_element_type=F32)
            return carry
        lax.fori_loop(0, n_blk, both_step, 0)

    p_copies = []
    for j in list(range(1, n_rep)) + [0]:
        at = pl.ds(pl.multiple_of(rep_at(j) * piece, piece), piece)
        if keep:
            def part_step(q, total):
                return total + jnp.dot(amat[q, at, :], with_ones(q), preferred_element_type=F32)
            total = lax.fori_loop(0, n_blk, part_step, jnp.zeros((piece, d_in + CB), F32))
        else:
            total = acc[at, :]
        pack(total, j)
        if j > 0:
            p_copies.append(
                send(psend.at[j], precv.at[j], p_ss, p_rs, j, rep=rep_at(j))
            )
    sent += p_copies

    gathered = psend[0, 0:piece, :].astype(F32)
    tail = psend[0, piece:, :].astype(F32)
    up_copy.wait()
    for copy, j in zip(p_copies, range(1, n_rep)):
        copy.wait_recv()
        gathered = gathered + precv[j, 0:piece, :].astype(F32)
        tail = tail + precv[j, piece:, :].astype(F32)
    degree_rows = [
        1.0 + tail[16 * i:16 * i + 1] + tail[16 * i + 8:16 * i + 9] for i in range(chunks)
    ]
    degree = jnp.concatenate([column(row) for row in degree_rows], axis=0)
    mixed = ((feat_ref[...].astype(F32) + gathered) / degree).astype(BF16)
    pre_act = jnp.dot(mixed, weight_ref[...], preferred_element_type=F32) + bias_ref[...]
    gate = jax.nn.sigmoid(pre_act)
    slope = gate * (1.0 + pre_act * (1.0 - gate))
    mask = jnp.concatenate(
        [column(mask_ref[pl.ds(z * chunks + i, 1), :].astype(F32)) for i in range(chunks)], axis=0
    )
    mask = jnp.concatenate([mask] * (hid // CB), axis=1)
    grad_pre = (upbuf[...].astype(F32) * mask * slope).astype(BF16)
    back = lax.dot_general(weight_ref[...], grad_pre, NT, preferred_element_type=F32)
    backs[0] = (back / jnp.concatenate(degree_rows, axis=1)).astype(BF16)
    b_copies = {
        j: send(backs.at[0], backs.at[j], b_ss, b_rs, j, rep=rep_at(j)) for j in range(1, n_rep)
    }
    sent += list(b_copies.values())

    act_ref[...] = (pre_act * gate).astype(BF16)
    weight_part = jnp.dot(
        mixed.astype(F32).T.astype(BF16), grad_pre, preferred_element_type=F32
    )
    bias_part = jnp.broadcast_to(
        jnp.sum(grad_pre.astype(F32), axis=0, keepdims=True), (8, hid)
    )
    for q in range(n_blk):
        w1s[q, 0:wch, :] = weight_part[q * wch:(q + 1) * wch]
        w1s[q, wch:, :] = bias_part
    w1r[b] = w1s[b]
    w1_copies = [
        send(w1s.at[blk_at(k)], w1r.at[b], w1_ss, w1_rs, k, blk=blk_at(k)) for k in range(1, n_blk)
    ]
    sent += w1_copies

    def reduce_first():
        for copy in w1_copies:
            copy.wait_recv()
        total = w1r[0]
        for q in range(1, n_blk):
            total = total + w1r[q]
        w2s[...] = total
        w2r[z] = total
        copies = [
            send(w2s, w2r.at[z], w2_ss, w2_rs, j, rep=rep_at(j)) for j in range(1, n_rep)
        ]
        return copies

    def reduce_second(copies):
        for copy in copies:
            copy.wait_recv()
        total = w2r[0]
        for q in range(1, n_rep):
            total = total + w2r[q]
        gb_ref[...] = total[wch:wch + 1]
        w3s[...] = total[0:wch]
        w3r[b] = total[0:wch]
        return [
            send(w3s, w3r.at[b], w3_ss, w3_rs, k, blk=blk_at(k)) for k in range(1, n_blk)
        ]

    order = [0] + list(range(1, n_rep))

    def rows_of(j):
        return pl.ds(pl.multiple_of(rep_at(n_rep - j) * piece, piece), piece)

    if keep:
        def first_step(q, carry):
            oacc[q] = jnp.dot(backs[0], amat[q, rows_of(0), :], preferred_element_type=F32)
            return carry
        lax.fori_loop(0, n_blk, first_step, 0)
        for j in order[1:-1]:
            b_copies[j].wait_recv()

            def more_step(q, carry, j=j):
                oacc[q] += jnp.dot(backs[j], amat[q, rows_of(j), :], preferred_element_type=F32)
                return carry
            lax.fori_loop(0, n_blk, more_step, 0)
        b_copies[order[-1]].wait_recv()
    else:
        for j in order[1:]:
            b_copies[j].wait_recv()

        def back_step(q, carry):
            build(q, 0)
            total = jnp.dot(backs[0], amat[0, rows_of(0), :], preferred_element_type=F32)
            for j in order[1:]:
                total = total + jnp.dot(backs[j], amat[0, rows_of(j), :], preferred_element_type=F32)
            oacc[q] = total
            return carry
        lax.fori_loop(0, n_blk, back_step, 0)

    g_copies = []
    for k in list(range(1, n_blk)) + [0]:
        q = blk_at(k)
        total = oacc[q]
        if keep:
            j = order[-1]
            total = total + jnp.dot(backs[j], amat[q, rows_of(j), :], preferred_element_type=F32)
        if k > 0:
            gsend[k] = total.astype(BF16)
            g_copies.append(send(gsend.at[k], grecv.at[k], g_ss, g_rs, k, blk=q))
        else:
            result = total + backs[0].astype(F32)
    sent += g_copies

    w2_copies = reduce_first()
    sent += w2_copies
    w3_copies = reduce_second(w2_copies)
    sent += w3_copies
    for k, copy in zip(range(1, n_blk), g_copies):
        copy.wait_recv()
        result = result + grecv[k].astype(F32)
    gf_ref[...] = result.T.astype(BF16)
    for copy in w3_copies:
        copy.wait_recv()
    for q in range(n_blk):
        gw_ref[q * wch:(q + 1) * wch, :] = w3r[q]
    for copy in sent:
        copy.wait_send()


def on_device(n_blk, n_rep, features, edge_rows, edge_cols, weight, bias, upstream, train_mask):
    piece, d_in = features.shape
    panel = upstream.shape[0]
    hid = weight.shape[1]
    wch = d_in // n_blk
    extra = 16 * (piece // CB)
    keep = panel * piece * n_blk * 2 <= 16 * 2**20
    sem = pltpu.SemaphoreType.DMA
    vmem = pl.BlockSpec(memory_space=pltpu.VMEM)
    act, gf, gw, gb = pl.pallas_call(
        functools.partial(kernel, n_blk, n_rep, keep),
        out_shape=(
            jax.ShapeDtypeStruct((piece, hid), BF16),
            jax.ShapeDtypeStruct((piece, d_in), BF16),
            jax.ShapeDtypeStruct((d_in, hid), F32),
            jax.ShapeDtypeStruct((1, hid), F32),
        ),
        in_specs=[vmem] * 6 + [pl.BlockSpec(memory_space=pl.ANY)],
        out_specs=(vmem,) * 4,
        scratch_shapes=[
            pltpu.VMEM((n_blk, piece, d_in), BF16),
            pltpu.VMEM((n_blk if keep else 1, panel, piece), BF16),
            pltpu.VMEM((8 if keep else panel, d_in + CB), F32),
            pltpu.VMEM((n_rep, piece + extra, d_in), BF16),
            pltpu.VMEM((n_rep, piece + extra, d_in), BF16),
            pltpu.VMEM((piece, hid), BF16),
            pltpu.VMEM((n_rep, d_in, piece), BF16),
            pltpu.VMEM((n_blk, d_in, piece), F32),
            pltpu.VMEM((n_blk, d_in, piece), BF16),
            pltpu.VMEM((n_blk, d_in, piece), BF16),
            pltpu.VMEM((n_blk, wch + 8, hid), F32),
            pltpu.VMEM((n_blk, wch + 8, hid), F32),
            pltpu.VMEM((wch + 8, hid), F32),
            pltpu.VMEM((n_rep, wch + 8, hid), F32),
            pltpu.VMEM((wch, hid), F32),
            pltpu.VMEM((n_blk, wch, hid), F32),
            sem((n_blk,)), sem((n_blk,)),
            sem((n_rep,)), sem((n_rep,)),
            sem((n_rep,)), sem((n_rep,)),
            sem((n_blk,)), sem((n_blk,)),
            sem((n_blk,)), sem((n_blk,)),
            sem((n_rep,)), sem((n_rep,)),
            sem((n_blk,)), sem((n_blk,)),
            sem,
        ],
        compiler_params=pltpu.CompilerParams(
            collective_id=0, has_side_effects=True, vmem_limit_bytes=48 * 2**20
        ),
    )(
        features, edge_rows, edge_cols, weight, bias.reshape(1, hid),
        train_mask.reshape(panel // CB, CB), upstream,
    )
    return act, gf, gw, gb.reshape(hid)


def solution(mesh):
    n_blk, n_rep = mesh.shape["blk"], mesh.shape["rep"]
    return jax.shard_map(
        functools.partial(on_device, n_blk, n_rep),
        mesh=mesh,
        in_specs=(
            P(("blk", "rep"), None),
            P("blk", None, "rep", None),
            P("blk", None, "rep", None),
            P(),
            P(),
            P("blk", None),
            P("blk"),
        ),
        out_specs=(P(("blk", "rep"), None), P(("blk", "rep"), None), P(), P()),
        check_vma=False,
    )
```

```python
import functools

import jax
import jax.numpy as jnp
from jax import lax
from jax.experimental import pallas as pl
from jax.experimental.pallas import tpu as pltpu
from jax.sharding import PartitionSpec as P

CB = 128
VMEM = 63 * 2**20
F32 = jnp.float32
BF16 = jnp.bfloat16
MESH = pl.DeviceIdType.MESH
NT = (((1,), (1,)), ((), ()))


def column(row):
    return jnp.broadcast_to(row, (CB, CB)).T


def partner(me, k, count):
    other, bit = 0, 1
    while bit < count:
        other += lax.rem(lax.div(me, bit) + (k // bit) % 2, 2) * bit
        bit *= 2
    return other


def one_hot(index, count):
    length = index.shape[-1]
    spot = lax.broadcasted_iota(jnp.int32, (count, length), 0)
    return jnp.where(spot == index, 1.0, 0.0).astype(BF16)


def kernel(
    n_blk, n_rep, keep,
    feat_hbm, rows_hbm, cols_hbm, weight_hbm, bias_hbm, mask_hbm, up_hbm,
    act_hbm, gf_hbm, gw_hbm, gb_hbm,
    feat_ref, rows_ref, cols_ref, weight_ref, bias_ref, mask_ref,
    act_ref, gf_ref, gw_ref, gb_ref, lowh, colh, fbuf, amat, acc, psend, precv, upbuf, backs, oacc, gsend, grecv,
    w1s, w1r, w2s, w2r, w3s, w3r,
    f_ss, f_rs, p_ss, p_rs, b_ss, b_rs, g_ss, g_rs, w1_ss, w1_rs, w2_ss, w2_rs, w3_ss, w3_rs, in_sem, out_sem,
):
    b = lax.axis_index("blk")
    z = lax.axis_index("rep")
    piece, d_in = feat_ref.shape
    panel = piece * n_rep
    hid = weight_ref.shape[1]
    chunks = piece // CB
    wch = d_in // n_blk

    def blk_at(k):
        return partner(b, k, n_blk)

    def rep_at(j):
        return partner(z, j, n_rep)

    def send(src, dst, ss, rs, i, **where):
        copy = pltpu.make_async_remote_copy(
            src_ref=src, dst_ref=dst, send_sem=ss.at[i], recv_sem=rs.at[i],
            device_id=where, device_id_type=MESH,
        )
        copy.start()
        return copy

    up_src = up_hbm.at[pl.ds(pl.multiple_of(z * piece, piece), piece)]
    loads = [
        pltpu.make_async_copy(src, dst, in_sem.at[i])
        for i, (src, dst) in enumerate((
            (feat_hbm, feat_ref), (rows_hbm, rows_ref), (cols_hbm, cols_ref),
            (weight_hbm, weight_ref), (bias_hbm, bias_ref), (mask_hbm, mask_ref), (up_src, upbuf),
        ))
    ]
    for load in loads:
        load.start()
    barrier = pltpu.get_barrier_semaphore()
    for k in range(1, n_blk):
        pl.semaphore_signal(barrier, inc=1, device_id={"blk": blk_at(k)}, device_id_type=MESH)
    for j in range(1, n_rep):
        pl.semaphore_signal(barrier, inc=1, device_id={"rep": rep_at(j)}, device_id_type=MESH)
    loads[0].wait()
    pl.semaphore_wait(barrier, n_blk + n_rep - 2)

    sent = []
    stored = []

    def store(src, dst):
        copy = pltpu.make_async_copy(src, dst, out_sem.at[len(stored)])
        copy.start()
        stored.append(copy)

    f_copies = [
        send(feat_ref, fbuf.at[b], f_ss, f_rs, k, blk=blk_at(k))
        for k in range(n_blk - 1, 0, -1)
    ]
    sent += f_copies
    fbuf[b] = feat_ref[...]
    for load in loads[1:3]:
        load.wait()

    def prepare(q, slot):
        for c in range(chunks):
            colh[slot, c] = one_hot(cols_ref[0, q, pl.ds(c, 1), :], CB)
            lowh[slot, c] = one_hot(rows_ref[0, q, pl.ds(c, 1), :] & (CB - 1), CB)

    def build(q, slot, first, count):
        made = []
        for c in range(chunks):
            rows = rows_ref[0, q, pl.ds(c, 1), :]
            high = jnp.broadcast_to(rows >> 7, (16, rows.shape[-1]))
            low_hot = lowh[slot, c]
            parts = []
            for h in range(count):
                picked = jnp.where(high == first + h, 1.0, 0.0).astype(BF16)
                parts.append(low_hot * jnp.concatenate([picked] * (CB // 16), axis=0))
            made.append(lax.dot_general(
                jnp.concatenate(parts, axis=0), colh[slot, c], NT, preferred_element_type=F32
            ).astype(BF16))
        at = pl.ds(pl.multiple_of(first * CB, CB), count * CB)
        made = jnp.concatenate(made, axis=1)
        amat[slot, at, :] = made
        return made

    def with_ones(q):
        return jnp.concatenate([fbuf[q], jnp.ones((piece, CB), BF16)], axis=1)

    def pack(total, slot):
        psend[slot, 0:piece, :] = total[:, :d_in].astype(BF16)
        counts = total[:, d_in:]
        tall = jnp.concatenate(
            [counts[i * CB:(i + 1) * CB].T[0:16] for i in range(chunks)], axis=0
        )
        top = tall.astype(BF16).astype(F32)
        line = lax.broadcasted_iota(jnp.int32, tall.shape, 0)
        psend[slot, piece:, :] = jnp.where(line % 16 < 8, top, tall - top).astype(BF16)

    order = ([2, 3] if n_rep == 4 else []) + [j for j in range(1, n_rep) if n_rep != 4 or j == 1]
    p_copies = []

    def piece_of(j):
        return pl.ds(pl.multiple_of(rep_at(j) * piece, piece), piece)

    def push(total, j):
        pack(total, j)
        if j > 0:
            p_copies.append(send(psend.at[j], precv.at[j], p_ss, p_rs, j, rep=rep_at(j)))

    blank = jnp.zeros((piece, d_in + CB), F32)
    if keep:
        def prepare_step(q, carry):
            prepare(q, q)
            return carry
        lax.fori_loop(0, n_blk, prepare_step, 0, unroll=2)
        lead = order[:2]
        for j in lead:
            def build_step(q, carry, j=j):
                build(q, q, rep_at(j) * chunks, chunks)
                return carry
            lax.fori_loop(0, n_blk, build_step, 0, unroll=4)
        for copy in f_copies:
            copy.wait_recv()
        for j in lead:
            def part_step(q, total, j=j):
                return total + jnp.dot(
                    amat[q, piece_of(j), :], with_ones(q), preferred_element_type=F32
                )
            push(lax.fori_loop(0, n_blk, part_step, blank, unroll=4), j)
        for j in order[2:] + [0]:
            def both_step(q, total, j=j):
                made = build(q, q, rep_at(j) * chunks, chunks)
                return total + jnp.dot(made, with_ones(q), preferred_element_type=F32)
            push(lax.fori_loop(0, n_blk, both_step, blank, unroll=4), j)
    else:
        for copy in f_copies:
            copy.wait_recv()
        acc[...] = jnp.zeros_like(acc)

        def whole_step(q, carry):
            prepare(q, 0)
            made = build(q, 0, 0, panel // CB)
            acc[...] += jnp.dot(made, with_ones(q), preferred_element_type=F32)
            return carry
        lax.fori_loop(0, n_blk, whole_step, 0)
        for j in order + [0]:
            push(acc[piece_of(j), :], j)
    sent += p_copies

    gathered = psend[0, 0:piece, :].astype(F32)
    tail = psend[0, piece:, :].astype(F32)
    for load in loads[3:]:
        load.wait()
    for copy, j in zip(p_copies, order):
        copy.wait_recv()
        gathered = gathered + precv[j, 0:piece, :].astype(F32)
        tail = tail + precv[j, piece:, :].astype(F32)
    degree_rows = [
        1.0 + tail[16 * i:16 * i + 1] + tail[16 * i + 8:16 * i + 9] for i in range(chunks)
    ]
    degree = jnp.concatenate([column(row) for row in degree_rows], axis=0)
    mixed = ((feat_ref[...].astype(F32) + gathered) / degree).astype(BF16)
    pre_act = jnp.dot(mixed, weight_ref[...], preferred_element_type=F32) + bias_ref[...]
    gate = jax.nn.sigmoid(pre_act)
    slope = gate * (1.0 + pre_act * (1.0 - gate))
    mask = jnp.concatenate(
        [column(mask_ref[pl.ds(z * chunks + i, 1), :].astype(F32)) for i in range(chunks)], axis=0
    )
    mask = jnp.concatenate([mask] * (hid // CB), axis=1)
    grad_pre = (upbuf[...].astype(F32) * mask * slope).astype(BF16)
    back = lax.dot_general(weight_ref[...], grad_pre, NT, preferred_element_type=F32)
    backs[0] = (back / jnp.concatenate(degree_rows, axis=1)).astype(BF16)
    b_copies = {
        j: send(backs.at[0], backs.at[j], b_ss, b_rs, j, rep=rep_at(j)) for j in order
    }
    sent += list(b_copies.values())

    act_ref[...] = (pre_act * gate).astype(BF16)
    store(act_ref, act_hbm)
    weight_part = jnp.dot(
        mixed.astype(F32).T.astype(BF16), grad_pre, preferred_element_type=F32
    )
    bias_part = jnp.broadcast_to(
        jnp.sum(grad_pre.astype(F32), axis=0, keepdims=True), (8, hid)
    )
    for q in range(n_blk):
        w1s[q, 0:wch, :] = weight_part[q * wch:(q + 1) * wch]
        w1s[q, wch:, :] = bias_part
    w1r[b] = w1s[b]
    w1_copies = [
        send(w1s.at[blk_at(k)], w1r.at[b], w1_ss, w1_rs, k, blk=blk_at(k)) for k in range(1, n_blk)
    ]
    sent += w1_copies

    def reduce_first():
        for copy in w1_copies:
            copy.wait_recv()
        total = w1r[0]
        for q in range(1, n_blk):
            total = total + w1r[q]
        w2s[...] = total
        w2r[z] = total
        copies = [
            send(w2s, w2r.at[z], w2_ss, w2_rs, j, rep=rep_at(j)) for j in range(1, n_rep)
        ]
        return copies

    def reduce_second(copies):
        for copy in copies:
            copy.wait_recv()
        total = w2r[0]
        for q in range(1, n_rep):
            total = total + w2r[q]
        gb_ref[...] = total[wch:wch + 1]
        store(gb_ref, gb_hbm)
        w3s[...] = total[0:wch]
        w3r[b] = total[0:wch]
        return [
            send(w3s, w3r.at[b], w3_ss, w3_rs, k, blk=blk_at(k)) for k in range(1, n_blk)
        ]

    arrive = list(range(1, n_rep))
    if keep:
        def first_step(q, carry):
            oacc[q] = jnp.dot(backs[0], amat[q, piece_of(0), :], preferred_element_type=F32)
            return carry
        lax.fori_loop(0, n_blk, first_step, 0, unroll=4)
        for j in arrive[:-1]:
            b_copies[j].wait_recv()

            def more_step(q, carry, j=j):
                oacc[q] += jnp.dot(backs[j], amat[q, piece_of(j), :], preferred_element_type=F32)
                return carry
            lax.fori_loop(0, n_blk, more_step, 0, unroll=4)
        b_copies[arrive[-1]].wait_recv()
    else:
        for j in arrive:
            b_copies[j].wait_recv()

        def back_step(q, carry):
            prepare(q, 0)
            build(q, 0, 0, panel // CB)
            total = jnp.dot(backs[0], amat[0, piece_of(0), :], preferred_element_type=F32)
            for j in arrive:
                total = total + jnp.dot(backs[j], amat[0, piece_of(j), :], preferred_element_type=F32)
            oacc[q] = total
            return carry
        lax.fori_loop(0, n_blk, back_step, 0)

    def source_sum(k):
        q = blk_at(k)
        total = oacc[q]
        if keep:
            j = arrive[-1]
            total = total + jnp.dot(backs[j], amat[q, piece_of(j), :], preferred_element_type=F32)
        return total

    g_copies = {}
    for k in list(range(n_blk - 1, 0, -2)):
        gsend[k] = source_sum(k).astype(BF16)
        g_copies[k] = send(gsend.at[k], grecv.at[k], g_ss, g_rs, k, blk=blk_at(1))
    w2_copies = reduce_first()
    sent += w2_copies
    for k in list(range(n_blk - 2, 0, -2)):
        total = source_sum(k)
        g_copies[k + 1].wait_recv()
        gsend[k] = (total + grecv[k + 1].astype(F32)).astype(BF16)
        g_copies[k] = send(gsend.at[k], grecv.at[k], g_ss, g_rs, k, blk=blk_at(k))
    result = source_sum(0) + backs[0].astype(F32)
    sent += list(g_copies.values())
    w3_copies = reduce_second(w2_copies)
    sent += w3_copies
    for k in [1] + list(range(2, n_blk, 2)):
        g_copies[k].wait_recv()
        result = result + grecv[k].astype(F32)
    gf_ref[...] = result.T.astype(BF16)
    store(gf_ref, gf_hbm)
    for copy in w3_copies:
        copy.wait_recv()
    for q in range(n_blk):
        gw_ref[q * wch:(q + 1) * wch, :] = w3r[q]
    store(gw_ref, gw_hbm)
    for copy in sent:
        copy.wait_send()
    for copy in stored:
        copy.wait()


def write_out(*refs):
    sems = refs[-1]
    count = (len(refs) - 1) // 2
    copies = [pltpu.make_async_copy(refs[i], refs[count + i], sems.at[i]) for i in range(count)]
    for copy in copies:
        copy.start()
    for copy in copies:
        copy.wait()


def on_device(n_blk, n_rep, features, edge_rows, edge_cols, weight, bias, upstream, train_mask):
    piece, d_in = features.shape
    panel = upstream.shape[0]
    hid = weight.shape[1]
    wch = d_in // n_blk
    extra = 16 * (piece // CB)
    keep = panel * piece * n_blk * 2 <= 16 * 2**20
    sem = pltpu.SemaphoreType.DMA
    anywhere = pl.BlockSpec(memory_space=pl.ANY)
    shapes = (
        jax.ShapeDtypeStruct((piece, hid), BF16),
        jax.ShapeDtypeStruct((piece, d_in), BF16),
        jax.ShapeDtypeStruct((d_in, hid), F32),
        jax.ShapeDtypeStruct((1, hid), F32),
    )
    slots = n_blk if keep else 1
    chunks, length = edge_rows.shape[2:]
    hbm = pl.BlockSpec(memory_space=pltpu.HBM)
    results = pl.pallas_call(
        functools.partial(kernel, n_blk, n_rep, keep),
        out_shape=shapes,
        in_specs=[hbm] * 7,
        out_specs=(anywhere,) * 4,
        scratch_shapes=[
            pltpu.VMEM((piece, d_in), BF16),
            pltpu.VMEM(edge_rows.shape, jnp.int32),
            pltpu.VMEM(edge_cols.shape, jnp.int32),
            pltpu.VMEM((d_in, hid), BF16),
            pltpu.VMEM((1, hid), F32),
            pltpu.VMEM((panel // CB, CB), jnp.int32),
            pltpu.VMEM((piece, hid), BF16),
            pltpu.VMEM((piece, d_in), BF16),
            pltpu.VMEM((d_in, hid), F32),
            pltpu.VMEM((1, hid), F32),
            pltpu.VMEM((slots, chunks, CB, length), BF16),
            pltpu.VMEM((slots, chunks, CB, length), BF16),
            pltpu.VMEM((n_blk, piece, d_in), BF16),
            pltpu.VMEM((slots, panel, piece), BF16),
            pltpu.VMEM((8 if keep else panel, d_in + CB), F32),
            pltpu.VMEM((n_rep, piece + extra, d_in), BF16),
            pltpu.VMEM((n_rep, piece + extra, d_in), BF16),
            pltpu.VMEM((piece, hid), BF16),
            pltpu.VMEM((n_rep, d_in, piece), BF16),
            pltpu.VMEM((n_blk, d_in, piece), F32),
            pltpu.VMEM((n_blk, d_in, piece), BF16),
            pltpu.VMEM((n_blk, d_in, piece), BF16),
            pltpu.VMEM((n_blk, wch + 8, hid), F32),
            pltpu.VMEM((n_blk, wch + 8, hid), F32),
            pltpu.VMEM((wch + 8, hid), F32),
            pltpu.VMEM((n_rep, wch + 8, hid), F32),
            pltpu.VMEM((wch, hid), F32),
            pltpu.VMEM((n_blk, wch, hid), F32),
            sem((n_blk,)), sem((n_blk,)),
            sem((n_rep,)), sem((n_rep,)),
            sem((n_rep,)), sem((n_rep,)),
            sem((n_blk,)), sem((n_blk,)),
            sem((n_blk,)), sem((n_blk,)),
            sem((n_rep,)), sem((n_rep,)),
            sem((n_blk,)), sem((n_blk,)),
            sem((7,)),
            sem((4,)),
        ],
        compiler_params=pltpu.CompilerParams(
            collective_id=0, has_side_effects=True, vmem_limit_bytes=VMEM
        ),
    )(
        features, edge_rows, edge_cols, weight, bias.reshape(1, hid),
        train_mask.reshape(panel // CB, CB), upstream,
    )
    act, gf, gw, gb = pl.pallas_call(
        write_out,
        out_shape=shapes,
        in_specs=[anywhere] * 4,
        out_specs=(hbm,) * 4,
        scratch_shapes=[sem((4,))],
        compiler_params=pltpu.CompilerParams(vmem_limit_bytes=VMEM),
    )(*results)
    return act, gf, gw, gb.reshape(hid)


def solution(mesh):
    n_blk, n_rep = mesh.shape["blk"], mesh.shape["rep"]
    return jax.shard_map(
        functools.partial(on_device, n_blk, n_rep),
        mesh=mesh,
        in_specs=(
            P(("blk", "rep"), None),
            P("blk", None, "rep", None),
            P("blk", None, "rep", None),
            P(),
            P(),
            P("blk", None),
            P("blk"),
        ),
        out_specs=(P(("blk", "rep"), None), P(("blk", "rep"), None), P(), P()),
        check_vma=False,
    )
```

```python
import functools

import jax
import jax.numpy as jnp
from jax import lax
from jax.experimental import pallas as pl
from jax.experimental.pallas import tpu as pltpu
from jax.sharding import PartitionSpec as P

CB = 128
VMEM = 48 * 2**20
F32 = jnp.float32
BF16 = jnp.bfloat16
MESH = pl.DeviceIdType.MESH
NT = (((1,), (1,)), ((), ()))


def column(row):
    return jnp.broadcast_to(row, (CB, CB)).T


def partner(me, k, count):
    other, bit = 0, 1
    while bit < count:
        other += lax.rem(lax.div(me, bit) + (k // bit) % 2, 2) * bit
        bit *= 2
    return other


def one_hot(index, count):
    length = index.shape[-1]
    spot = lax.broadcasted_iota(jnp.int32, (count, length), 0)
    return jnp.where(spot == index, 1.0, 0.0).astype(BF16)


def kernel(
    n_blk, n_rep, keep,
    feat_hbm, rows_hbm, cols_hbm, weight_hbm, bias_hbm, mask_hbm, up_hbm,
    act_ref, gf_ref, gw_ref, gb_ref,
    feat_ref, rows_ref, cols_ref, weight_ref, bias_ref, mask_ref,
    lowh, colh, fbuf, amat, acc, psend, precv, upbuf, backs, oacc, gsend, grecv,
    w1s, w1r, w2s, w2r, w3s, w3r,
    f_ss, f_rs, p_ss, p_rs, b_ss, b_rs, g_ss, g_rs, w1_ss, w1_rs, w2_ss, w2_rs, w3_ss, w3_rs, in_sem,
):
    b = lax.axis_index("blk")
    z = lax.axis_index("rep")
    piece, d_in = feat_ref.shape
    panel = piece * n_rep
    hid = weight_ref.shape[1]
    chunks = piece // CB
    wch = d_in // n_blk

    def blk_at(k):
        return partner(b, k, n_blk)

    def rep_at(j):
        return partner(z, j, n_rep)

    def send(src, dst, ss, rs, i, **where):
        copy = pltpu.make_async_remote_copy(
            src_ref=src, dst_ref=dst, send_sem=ss.at[i], recv_sem=rs.at[i],
            device_id=where, device_id_type=MESH,
        )
        copy.start()
        return copy

    up_src = up_hbm.at[pl.ds(pl.multiple_of(z * piece, piece), piece)]
    loads = [
        pltpu.make_async_copy(src, dst, in_sem.at[i])
        for i, (src, dst) in enumerate((
            (feat_hbm, feat_ref), (rows_hbm, rows_ref), (cols_hbm, cols_ref),
            (weight_hbm, weight_ref), (bias_hbm, bias_ref), (mask_hbm, mask_ref), (up_src, upbuf),
        ))
    ]
    for load in loads:
        load.start()
    barrier = pltpu.get_barrier_semaphore()
    for k in range(1, n_blk):
        pl.semaphore_signal(barrier, inc=1, device_id={"blk": blk_at(k)}, device_id_type=MESH)
    for j in range(1, n_rep):
        pl.semaphore_signal(barrier, inc=1, device_id={"rep": rep_at(j)}, device_id_type=MESH)
    loads[0].wait()
    pl.semaphore_wait(barrier, n_blk + n_rep - 2)

    sent = []
    even = list(range(n_blk - 2, 0, -2))
    f_copies = {
        k: send(feat_ref, fbuf.at[b], f_ss, f_rs, k, blk=blk_at(k)) for k in even + [1]
    }

    def hand_on():
        for k in even:
            f_copies[k].wait_recv()
            slot = fbuf.at[blk_at(k)]
            f_copies[k + 1] = send(slot, slot, f_ss, f_rs, k + 1, blk=blk_at(1))

    def all_here():
        for k in range(1, n_blk, 2):
            f_copies[k].wait_recv()

    fbuf[b] = feat_ref[...]
    for load in loads[1:3]:
        load.wait()

    def prepare(q, slot):
        for c in range(chunks):
            colh[slot, c] = one_hot(cols_ref[0, q, pl.ds(c, 1), :], CB)
            lowh[slot, c] = one_hot(rows_ref[0, q, pl.ds(c, 1), :] & (CB - 1), CB)

    def build(q, slot, first, count):
        made = []
        for c in range(chunks):
            rows = rows_ref[0, q, pl.ds(c, 1), :]
            high = jnp.broadcast_to(rows >> 7, (16, rows.shape[-1]))
            low_hot = lowh[slot, c]
            parts = []
            for h in range(count):
                picked = jnp.where(high == first + h, 1.0, 0.0).astype(BF16)
                parts.append(low_hot * jnp.concatenate([picked] * (CB // 16), axis=0))
            made.append(lax.dot_general(
                jnp.concatenate(parts, axis=0), colh[slot, c], NT, preferred_element_type=F32
            ).astype(BF16))
        at = pl.ds(pl.multiple_of(first * CB, CB), count * CB)
        made = jnp.concatenate(made, axis=1)
        amat[slot, at, :] = made
        return made

    def with_ones(q):
        return jnp.concatenate([fbuf[q], jnp.ones((piece, CB), BF16)], axis=1)

    def pack(total, slot, more=None):
        part = total[:, :d_in].astype(BF16)
        if more is not None:
            part = (part.astype(F32) + more[0:piece].astype(F32)).astype(BF16)
        psend[slot, 0:piece, :] = part
        counts = total[:, d_in:]
        tall = jnp.concatenate(
            [counts[i * CB:(i + 1) * CB].T[0:16] for i in range(chunks)], axis=0
        )
        if more is not None:
            extra = more[piece:].astype(F32)
            pairs = [
                extra[16 * i:16 * i + 8] + extra[16 * i + 8:16 * i + 16] for i in range(chunks)
            ]
            tall = tall + jnp.concatenate([x for pair in pairs for x in (pair, pair)], axis=0)
        top = tall.astype(BF16).astype(F32)
        line = lax.broadcasted_iota(jnp.int32, tall.shape, 0)
        psend[slot, piece:, :] = jnp.where(line % 16 < 8, top, tall - top).astype(BF16)

    odd_rep = list(range(n_rep - 1, 1, -2))
    even_rep = list(range(n_rep - 2, 0, -2))
    order = even_rep + odd_rep + [1]
    p_copies = {}

    def piece_of(j):
        return pl.ds(pl.multiple_of(rep_at(j) * piece, piece), piece)

    def push(total, j):
        if j in even_rep:
            p_copies[j + 1].wait_recv()
            pack(total, j, precv[j + 1])
        else:
            pack(total, j)
        if j > 0:
            to = rep_at(1 if j in odd_rep else j)
            p_copies[j] = send(psend.at[j], precv.at[j], p_ss, p_rs, j, rep=to)

    blank = jnp.zeros((piece, d_in + CB), F32)
    if keep:
        def prepare_step(q, carry):
            prepare(q, q)
            return carry
        lax.fori_loop(0, n_blk, prepare_step, 0, unroll=2)
        held = None
        turns = odd_rep + even_rep + [1, 0]
        lead = turns[:2]
        for j in lead:
            if j == lead[1]:
                hand_on()

            def build_step(q, carry, j=j):
                build(q, q, rep_at(j) * chunks, chunks)
                return carry
            lax.fori_loop(0, n_blk, build_step, 0, unroll=4)
        all_here()
        for j in lead:
            def part_step(q, total, j=j):
                return total + jnp.dot(
                    amat[q, piece_of(j), :], with_ones(q), preferred_element_type=F32
                )
            total = lax.fori_loop(0, n_blk, part_step, blank, unroll=4)
            if j in even_rep:
                held = (total, j)
            else:
                push(total, j)
        for j in turns[2:]:
            def both_step(q, total, j=j):
                made = build(q, q, rep_at(j) * chunks, chunks)
                return total + jnp.dot(made, with_ones(q), preferred_element_type=F32)
            push(lax.fori_loop(0, n_blk, both_step, blank, unroll=4), j)
            if held is not None:
                push(*held)
                held = None
    else:
        hand_on()
        all_here()
        acc[...] = jnp.zeros_like(acc)

        def whole_step(q, carry):
            prepare(q, 0)
            made = build(q, 0, 0, panel // CB)
            acc[...] += jnp.dot(made, with_ones(q), preferred_element_type=F32)
            return carry
        lax.fori_loop(0, n_blk, whole_step, 0)
        for j in odd_rep + even_rep + [1, 0]:
            push(acc[piece_of(j), :], j)
    sent += list(f_copies.values()) + list(p_copies.values())

    gathered = psend[0, 0:piece, :].astype(F32)
    tail = psend[0, piece:, :].astype(F32)
    for load in loads[3:]:
        load.wait()
    for j in even_rep + [1]:
        p_copies[j].wait_recv()
        gathered = gathered + precv[j, 0:piece, :].astype(F32)
        tail = tail + precv[j, piece:, :].astype(F32)
    degree_rows = [
        1.0 + tail[16 * i:16 * i + 1] + tail[16 * i + 8:16 * i + 9] for i in range(chunks)
    ]
    degree = jnp.concatenate([column(row) for row in degree_rows], axis=0)
    mixed = ((feat_ref[...].astype(F32) + gathered) / degree).astype(BF16)
    pre_act = jnp.dot(mixed, weight_ref[...], preferred_element_type=F32) + bias_ref[...]
    gate = jax.nn.sigmoid(pre_act)
    slope = gate * (1.0 + pre_act * (1.0 - gate))
    mask = jnp.concatenate(
        [column(mask_ref[pl.ds(z * chunks + i, 1), :].astype(F32)) for i in range(chunks)], axis=0
    )
    mask = jnp.concatenate([mask] * (hid // CB), axis=1)
    grad_pre = (upbuf[...].astype(F32) * mask * slope).astype(BF16)
    back = lax.dot_general(weight_ref[...], grad_pre, NT, preferred_element_type=F32)
    backs[0] = (back / jnp.concatenate(degree_rows, axis=1)).astype(BF16)
    b_copies = {
        j: send(backs.at[0], backs.at[j], b_ss, b_rs, j, rep=rep_at(j)) for j in order
    }
    sent += list(b_copies.values())

    act_ref[...] = (pre_act * gate).astype(BF16)
    weight_part = jnp.dot(
        mixed.astype(F32).T.astype(BF16), grad_pre, preferred_element_type=F32
    )
    bias_part = jnp.broadcast_to(
        jnp.sum(grad_pre.astype(F32), axis=0, keepdims=True), (8, hid)
    )
    for q in range(n_blk):
        w1s[q, 0:wch, :] = weight_part[q * wch:(q + 1) * wch]
        w1s[q, wch:, :] = bias_part
    w1r[b] = w1s[b]
    w1_copies = [
        send(w1s.at[blk_at(k)], w1r.at[b], w1_ss, w1_rs, k, blk=blk_at(k)) for k in range(1, n_blk)
    ]
    sent += w1_copies

    def reduce_first():
        for copy in w1_copies:
            copy.wait_recv()
        total = w1r[0]
        for q in range(1, n_blk):
            total = total + w1r[q]
        w2s[...] = total
        w2r[z] = total
        copies = [
            send(w2s, w2r.at[z], w2_ss, w2_rs, j, rep=rep_at(j)) for j in range(1, n_rep)
        ]
        return copies

    def reduce_second(copies):
        for copy in copies:
            copy.wait_recv()
        total = w2r[0]
        for q in range(1, n_rep):
            total = total + w2r[q]
        gb_ref[...] = total[wch:wch + 1]
        w3s[...] = total[0:wch]
        w3r[b] = total[0:wch]
        return {k: send(w3s, w3r.at[b], w3_ss, w3_rs, k, blk=blk_at(k)) for k in even + [1]}

    def hand_on_weights(copies):
        for k in even:
            copies[k].wait_recv()
            slot = w3r.at[blk_at(k)]
            copies[k + 1] = send(slot, slot, w3_ss, w3_rs, k + 1, blk=blk_at(1))

    arrive = list(range(1, n_rep))
    if keep:
        def first_step(q, carry):
            oacc[q] = jnp.dot(backs[0], amat[q, piece_of(0), :], preferred_element_type=F32)
            return carry
        lax.fori_loop(0, n_blk, first_step, 0, unroll=4)
        for j in arrive[:-1]:
            b_copies[j].wait_recv()

            def more_step(q, carry, j=j):
                oacc[q] += jnp.dot(backs[j], amat[q, piece_of(j), :], preferred_element_type=F32)
                return carry
            lax.fori_loop(0, n_blk, more_step, 0, unroll=4)
        w2_copies = reduce_first()
        b_copies[arrive[-1]].wait_recv()
    else:
        w2_copies = reduce_first()
        for j in arrive:
            b_copies[j].wait_recv()

        def back_step(q, carry):
            prepare(q, 0)
            build(q, 0, 0, panel // CB)
            total = jnp.dot(backs[0], amat[0, piece_of(0), :], preferred_element_type=F32)
            for j in arrive:
                total = total + jnp.dot(backs[j], amat[0, piece_of(j), :], preferred_element_type=F32)
            oacc[q] = total
            return carry
        lax.fori_loop(0, n_blk, back_step, 0)

    def source_sum(k):
        q = blk_at(k)
        total = oacc[q]
        if keep:
            j = arrive[-1]
            total = total + jnp.dot(backs[j], amat[q, piece_of(j), :], preferred_element_type=F32)
        return total

    g_copies = {}
    for k in list(range(n_blk - 1, 0, -2)):
        gsend[k] = source_sum(k).astype(BF16)
        g_copies[k] = send(gsend.at[k], grecv.at[k], g_ss, g_rs, k, blk=blk_at(1))
    w3_copies = reduce_second(w2_copies)
    for k in even:
        total = source_sum(k)
        g_copies[k + 1].wait_recv()
        gsend[k] = (total + grecv[k + 1].astype(F32)).astype(BF16)
        g_copies[k] = send(gsend.at[k], grecv.at[k], g_ss, g_rs, k, blk=blk_at(k))
    result = source_sum(0) + backs[0].astype(F32)
    hand_on_weights(w3_copies)
    sent += list(g_copies.values()) + w2_copies + list(w3_copies.values())
    for k in [1] + list(range(2, n_blk, 2)):
        g_copies[k].wait_recv()
        result = result + grecv[k].astype(F32)
    gf_ref[...] = result.T.astype(BF16)
    for k in range(1, n_blk, 2):
        w3_copies[k].wait_recv()
    for q in range(n_blk):
        gw_ref[q * wch:(q + 1) * wch, :] = w3r[q]
    for copy in sent:
        copy.wait_send()


def write_out(*refs):
    sems = refs[-1]
    count = (len(refs) - 1) // 2
    copies = [pltpu.make_async_copy(refs[i], refs[count + i], sems.at[i]) for i in range(count)]
    for copy in copies:
        copy.start()
    for copy in copies:
        copy.wait()


def on_device(n_blk, n_rep, features, edge_rows, edge_cols, weight, bias, upstream, train_mask):
    piece, d_in = features.shape
    panel = upstream.shape[0]
    hid = weight.shape[1]
    wch = d_in // n_blk
    extra = 16 * (piece // CB)
    keep = panel * piece * n_blk * 2 <= 16 * 2**20
    sem = pltpu.SemaphoreType.DMA
    anywhere = pl.BlockSpec(memory_space=pl.ANY)
    shapes = (
        jax.ShapeDtypeStruct((piece, hid), BF16),
        jax.ShapeDtypeStruct((piece, d_in), BF16),
        jax.ShapeDtypeStruct((d_in, hid), F32),
        jax.ShapeDtypeStruct((1, hid), F32),
    )
    slots = n_blk if keep else 1
    chunks, length = edge_rows.shape[2:]
    hbm = pl.BlockSpec(memory_space=pltpu.HBM)
    results = pl.pallas_call(
        functools.partial(kernel, n_blk, n_rep, keep),
        out_shape=shapes,
        in_specs=[hbm] * 7,
        out_specs=(pl.BlockSpec(memory_space=pltpu.VMEM),) * 4,
        scratch_shapes=[
            pltpu.VMEM((piece, d_in), BF16),
            pltpu.VMEM(edge_rows.shape, jnp.int32),
            pltpu.VMEM(edge_cols.shape, jnp.int32),
            pltpu.VMEM((d_in, hid), BF16),
            pltpu.VMEM((1, hid), F32),
            pltpu.VMEM((panel // CB, CB), jnp.int32),
            pltpu.VMEM((slots, chunks, CB, length), BF16),
            pltpu.VMEM((slots, chunks, CB, length), BF16),
            pltpu.VMEM((n_blk, piece, d_in), BF16),
            pltpu.VMEM((slots, panel, piece), BF16),
            pltpu.VMEM((8 if keep else panel, d_in + CB), F32),
            pltpu.VMEM((n_rep, piece + extra, d_in), BF16),
            pltpu.VMEM((n_rep, piece + extra, d_in), BF16),
            pltpu.VMEM((piece, hid), BF16),
            pltpu.VMEM((n_rep, d_in, piece), BF16),
            pltpu.VMEM((n_blk, d_in, piece), F32),
            pltpu.VMEM((n_blk, d_in, piece), BF16),
            pltpu.VMEM((n_blk, d_in, piece), BF16),
            pltpu.VMEM((n_blk, wch + 8, hid), F32),
            pltpu.VMEM((n_blk, wch + 8, hid), F32),
            pltpu.VMEM((wch + 8, hid), F32),
            pltpu.VMEM((n_rep, wch + 8, hid), F32),
            pltpu.VMEM((wch, hid), F32),
            pltpu.VMEM((n_blk, wch, hid), F32),
            sem((n_blk,)), sem((n_blk,)),
            sem((n_rep,)), sem((n_rep,)),
            sem((n_rep,)), sem((n_rep,)),
            sem((n_blk,)), sem((n_blk,)),
            sem((n_blk,)), sem((n_blk,)),
            sem((n_rep,)), sem((n_rep,)),
            sem((n_blk,)), sem((n_blk,)),
            sem((7,)),
        ],
        compiler_params=pltpu.CompilerParams(
            collective_id=0, has_side_effects=True, vmem_limit_bytes=VMEM
        ),
    )(
        *[pltpu.with_memory_space_constraint(x, pltpu.HBM) for x in (
            features, edge_rows, edge_cols, weight, bias.reshape(1, hid),
            train_mask.reshape(panel // CB, CB), upstream,
        )]
    )
    act, gf, gw, gb = pl.pallas_call(
        write_out,
        out_shape=shapes,
        in_specs=[anywhere] * 4,
        out_specs=(hbm,) * 4,
        scratch_shapes=[sem((4,))],
        compiler_params=pltpu.CompilerParams(vmem_limit_bytes=VMEM),
    )(*results)
    return act, gf, gw, gb.reshape(hid)


def solution(mesh):
    n_blk, n_rep = mesh.shape["blk"], mesh.shape["rep"]
    return jax.shard_map(
        functools.partial(on_device, n_blk, n_rep),
        mesh=mesh,
        in_specs=(
            P(("blk", "rep"), None),
            P("blk", None, "rep", None),
            P("blk", None, "rep", None),
            P(),
            P(),
            P("blk", None),
            P("blk"),
        ),
        out_specs=(P(("blk", "rep"), None), P(("blk", "rep"), None), P(), P()),
        check_vma=False,
    )
```

```python
import functools

import jax
import jax.numpy as jnp
from jax import lax
from jax.experimental import pallas as pl
from jax.experimental.pallas import tpu as pltpu
from jax.sharding import PartitionSpec as P

CB = 128
VMEM = 48 * 2**20
F32 = jnp.float32
BF16 = jnp.bfloat16
MESH = pl.DeviceIdType.MESH
NT = (((1,), (1,)), ((), ()))


def column(row):
    return jnp.broadcast_to(row, (CB, CB)).T


def partner(me, k, count):
    other, bit = 0, 1
    while bit < count:
        other += lax.rem(lax.div(me, bit) + (k // bit) % 2, 2) * bit
        bit *= 2
    return other


def one_hot(index, count):
    length = index.shape[-1]
    spot = lax.broadcasted_iota(jnp.int32, (count, length), 0)
    return jnp.where(spot == index, 1.0, 0.0).astype(BF16)


def kernel(
    n_blk, n_rep, keep,
    feat_hbm, rows_hbm, cols_hbm, weight_hbm, bias_hbm, mask_hbm, up_hbm,
    act_ref, gf_ref, gw_ref, gb_ref,
    feat_ref, rows_ref, cols_ref, weight_ref, bias_ref, mask_ref,
    fbuf, amat, acc, psend, precv, upbuf, backs, oacc, gsend, grecv,
    w1s, w1r, w2s, w2r, w3s, w3r,
    f_ss, f_rs, p_ss, p_rs, b_ss, b_rs, g_ss, g_rs, w1_ss, w1_rs, w2_ss, w2_rs, w3_ss, w3_rs, in_sem,
):
    b = lax.axis_index("blk")
    z = lax.axis_index("rep")
    piece, d_in = feat_ref.shape
    panel = piece * n_rep
    hid = weight_ref.shape[1]
    chunks = piece // CB
    wch = d_in // n_blk

    def blk_at(k):
        return partner(b, k, n_blk)

    def rep_at(j):
        return partner(z, j, n_rep)

    def send(src, dst, ss, rs, i, **where):
        copy = pltpu.make_async_remote_copy(
            src_ref=src, dst_ref=dst, send_sem=ss.at[i], recv_sem=rs.at[i],
            device_id=where, device_id_type=MESH,
        )
        copy.start()
        return copy

    up_src = up_hbm.at[pl.ds(pl.multiple_of(z * piece, piece), piece)]
    loads = [
        pltpu.make_async_copy(src, dst, in_sem.at[i])
        for i, (src, dst) in enumerate((
            (feat_hbm, feat_ref), (rows_hbm, rows_ref), (cols_hbm, cols_ref),
            (weight_hbm, weight_ref), (bias_hbm, bias_ref), (mask_hbm, mask_ref), (up_src, upbuf),
        ))
    ]
    for load in loads:
        load.start()
    barrier = pltpu.get_barrier_semaphore()
    for k in range(1, n_blk):
        pl.semaphore_signal(barrier, inc=1, device_id={"blk": blk_at(k)}, device_id_type=MESH)
    for j in range(1, n_rep):
        pl.semaphore_signal(barrier, inc=1, device_id={"rep": rep_at(j)}, device_id_type=MESH)
    loads[0].wait()
    pl.semaphore_wait(barrier, n_blk + n_rep - 2)

    sent = []
    even = list(range(n_blk - 2, 0, -2))
    f_copies = {
        k: send(feat_ref, fbuf.at[b], f_ss, f_rs, k, blk=blk_at(k)) for k in even + [1]
    }

    def hand_on():
        for k in even:
            f_copies[k].wait_recv()
            slot = fbuf.at[blk_at(k)]
            f_copies[k + 1] = send(slot, slot, f_ss, f_rs, k + 1, blk=blk_at(1))

    def all_here():
        for k in range(1, n_blk, 2):
            f_copies[k].wait_recv()

    fbuf[b] = feat_ref[...]
    for load in loads[1:3]:
        load.wait()

    def build(q, slot):
        for c in range(chunks):
            rows = rows_ref[0, q, pl.ds(c, 1), :]
            cols = cols_ref[0, q, pl.ds(c, 1), :]
            wide_hot = one_hot(cols + (rows & CB), 2 * CB)
            low_hot = one_hot(rows & (CB - 1), CB)
            pair = jnp.broadcast_to(rows >> 8, (16, rows.shape[-1]))
            parts = []
            for h in range(panel // (2 * CB)):
                picked = jnp.where(pair == h, 1.0, 0.0).astype(BF16)
                parts.append(low_hot * jnp.concatenate([picked] * (CB // 16), axis=0))
            made = lax.dot_general(
                jnp.concatenate(parts, axis=0), wide_hot, NT, preferred_element_type=F32
            ).astype(BF16)
            for h in range(panel // CB):
                amat[slot, h * CB:(h + 1) * CB, c * CB:(c + 1) * CB] = made[
                    (h // 2) * CB:(h // 2 + 1) * CB, (h % 2) * CB:(h % 2 + 1) * CB
                ]

    def with_ones(q):
        return jnp.concatenate([fbuf[q], jnp.ones((piece, CB), BF16)], axis=1)

    def pack(total, slot, more=None):
        part = total[:, :d_in].astype(BF16)
        if more is not None:
            part = (part.astype(F32) + more[0:piece].astype(F32)).astype(BF16)
        psend[slot, 0:piece, :] = part
        counts = total[:, d_in:]
        tall = jnp.concatenate(
            [counts[i * CB:(i + 1) * CB].T[0:16] for i in range(chunks)], axis=0
        )
        if more is not None:
            extra = more[piece:].astype(F32)
            pairs = [
                extra[16 * i:16 * i + 8] + extra[16 * i + 8:16 * i + 16] for i in range(chunks)
            ]
            tall = tall + jnp.concatenate([x for pair in pairs for x in (pair, pair)], axis=0)
        top = tall.astype(BF16).astype(F32)
        line = lax.broadcasted_iota(jnp.int32, tall.shape, 0)
        psend[slot, piece:, :] = jnp.where(line % 16 < 8, top, tall - top).astype(BF16)

    odd_rep = list(range(n_rep - 1, 1, -2))
    even_rep = list(range(n_rep - 2, 0, -2))
    order = even_rep + odd_rep + [1]
    p_copies = {}

    def piece_of(j):
        return pl.ds(pl.multiple_of(rep_at(j) * piece, piece), piece)

    def push(total, j):
        if j in even_rep:
            p_copies[j + 1].wait_recv()
            pack(total, j, precv[j + 1])
        else:
            pack(total, j)
        if j > 0:
            to = rep_at(1 if j in odd_rep else j)
            p_copies[j] = send(psend.at[j], precv.at[j], p_ss, p_rs, j, rep=to)

    blank = jnp.zeros((piece, d_in + CB), F32)
    if keep:
        def build_step(q, carry):
            build(q, q)
            return carry
        half = n_blk // 2
        lax.fori_loop(0, half, build_step, 0, unroll=2)
        hand_on()
        lax.fori_loop(half, n_blk, build_step, 0, unroll=2)
        all_here()
        for j in odd_rep + [1] + even_rep + [0]:
            def part_step(q, total, j=j):
                return total + jnp.dot(
                    amat[q, piece_of(j), :], with_ones(q), preferred_element_type=F32
                )
            push(lax.fori_loop(0, n_blk, part_step, blank, unroll=4), j)
    else:
        hand_on()
        all_here()
        acc[...] = jnp.zeros_like(acc)

        def whole_step(q, carry):
            build(q, 0)
            acc[...] += jnp.dot(amat[0], with_ones(q), preferred_element_type=F32)
            return carry
        lax.fori_loop(0, n_blk, whole_step, 0)
        for j in odd_rep + even_rep + [1, 0]:
            push(acc[piece_of(j), :], j)
    sent += list(f_copies.values()) + list(p_copies.values())

    gathered = psend[0, 0:piece, :].astype(F32)
    tail = psend[0, piece:, :].astype(F32)
    for load in loads[3:]:
        load.wait()
    for j in even_rep + [1]:
        p_copies[j].wait_recv()
        gathered = gathered + precv[j, 0:piece, :].astype(F32)
        tail = tail + precv[j, piece:, :].astype(F32)
    degree_rows = [
        1.0 + tail[16 * i:16 * i + 1] + tail[16 * i + 8:16 * i + 9] for i in range(chunks)
    ]
    degree = jnp.concatenate([column(row) for row in degree_rows], axis=0)
    mixed = ((feat_ref[...].astype(F32) + gathered) / degree).astype(BF16)
    pre_act = jnp.dot(mixed, weight_ref[...], preferred_element_type=F32) + bias_ref[...]
    gate = jax.nn.sigmoid(pre_act)
    slope = gate * (1.0 + pre_act * (1.0 - gate))
    mask = jnp.concatenate(
        [column(mask_ref[pl.ds(z * chunks + i, 1), :].astype(F32)) for i in range(chunks)], axis=0
    )
    mask = jnp.concatenate([mask] * (hid // CB), axis=1)
    grad_pre = (upbuf[...].astype(F32) * mask * slope).astype(BF16)
    back = lax.dot_general(weight_ref[...], grad_pre, NT, preferred_element_type=F32)
    backs[0] = (back / jnp.concatenate(degree_rows, axis=1)).astype(BF16)
    b_copies = {
        j: send(backs.at[0], backs.at[j], b_ss, b_rs, j, rep=rep_at(j)) for j in order
    }
    sent += list(b_copies.values())

    act_ref[...] = (pre_act * gate).astype(BF16)
    weight_part = jnp.dot(
        mixed.astype(F32).T.astype(BF16), grad_pre, preferred_element_type=F32
    )
    bias_part = jnp.broadcast_to(
        jnp.sum(grad_pre.astype(F32), axis=0, keepdims=True), (8, hid)
    )
    for q in range(n_blk):
        w1s[q, 0:wch, :] = weight_part[q * wch:(q + 1) * wch]
        w1s[q, wch:, :] = bias_part
    w1r[b] = w1s[b]
    w1_copies = [
        send(w1s.at[blk_at(k)], w1r.at[b], w1_ss, w1_rs, k, blk=blk_at(k)) for k in range(1, n_blk)
    ]
    sent += w1_copies

    def reduce_first():
        for copy in w1_copies:
            copy.wait_recv()
        total = w1r[0]
        for q in range(1, n_blk):
            total = total + w1r[q]
        w2s[...] = total
        w2r[z] = total
        copies = [
            send(w2s, w2r.at[z], w2_ss, w2_rs, j, rep=rep_at(j)) for j in range(1, n_rep)
        ]
        return copies

    def reduce_second(copies):
        for copy in copies:
            copy.wait_recv()
        total = w2r[0]
        for q in range(1, n_rep):
            total = total + w2r[q]
        gb_ref[...] = total[wch:wch + 1]
        w3s[...] = total[0:wch]
        w3r[b] = total[0:wch]
        return {k: send(w3s, w3r.at[b], w3_ss, w3_rs, k, blk=blk_at(k)) for k in even + [1]}

    def hand_on_weights(copies):
        for k in even:
            copies[k].wait_recv()
            slot = w3r.at[blk_at(k)]
            copies[k + 1] = send(slot, slot, w3_ss, w3_rs, k + 1, blk=blk_at(1))

    arrive = list(range(1, n_rep))
    if keep:
        def first_step(q, carry):
            oacc[q] = jnp.dot(backs[0], amat[q, piece_of(0), :], preferred_element_type=F32)
            return carry
        lax.fori_loop(0, n_blk, first_step, 0, unroll=4)
        for j in arrive[:-1]:
            b_copies[j].wait_recv()

            def more_step(q, carry, j=j):
                oacc[q] += jnp.dot(backs[j], amat[q, piece_of(j), :], preferred_element_type=F32)
                return carry
            lax.fori_loop(0, n_blk, more_step, 0, unroll=4)
        w2_copies = reduce_first()
        b_copies[arrive[-1]].wait_recv()
    else:
        w2_copies = reduce_first()
        for j in arrive:
            b_copies[j].wait_recv()

        def back_step(q, carry):
            build(q, 0)
            total = jnp.dot(backs[0], amat[0, piece_of(0), :], preferred_element_type=F32)
            for j in arrive:
                total = total + jnp.dot(backs[j], amat[0, piece_of(j), :], preferred_element_type=F32)
            oacc[q] = total
            return carry
        lax.fori_loop(0, n_blk, back_step, 0)

    def source_sum(k):
        q = blk_at(k)
        total = oacc[q]
        if keep:
            j = arrive[-1]
            total = total + jnp.dot(backs[j], amat[q, piece_of(j), :], preferred_element_type=F32)
        return total

    g_copies = {}
    for k in list(range(n_blk - 1, 0, -2)):
        gsend[k] = source_sum(k).astype(BF16)
        g_copies[k] = send(gsend.at[k], grecv.at[k], g_ss, g_rs, k, blk=blk_at(1))
    w3_copies = reduce_second(w2_copies)
    for k in even:
        total = source_sum(k)
        g_copies[k + 1].wait_recv()
        gsend[k] = (total + grecv[k + 1].astype(F32)).astype(BF16)
        g_copies[k] = send(gsend.at[k], grecv.at[k], g_ss, g_rs, k, blk=blk_at(k))
    result = source_sum(0) + backs[0].astype(F32)
    hand_on_weights(w3_copies)
    sent += list(g_copies.values()) + w2_copies + list(w3_copies.values())
    for k in [1] + list(range(2, n_blk, 2)):
        g_copies[k].wait_recv()
        result = result + grecv[k].astype(F32)
    gf_ref[...] = result.T.astype(BF16)
    for k in range(1, n_blk, 2):
        w3_copies[k].wait_recv()
    for q in range(n_blk):
        gw_ref[q * wch:(q + 1) * wch, :] = w3r[q]
    for copy in sent:
        copy.wait_send()


def write_out(*refs):
    sems = refs[-1]
    count = (len(refs) - 1) // 2
    copies = [pltpu.make_async_copy(refs[i], refs[count + i], sems.at[i]) for i in range(count)]
    for copy in copies:
        copy.start()
    for copy in copies:
        copy.wait()


def on_device(n_blk, n_rep, features, edge_rows, edge_cols, weight, bias, upstream, train_mask):
    piece, d_in = features.shape
    panel = upstream.shape[0]
    hid = weight.shape[1]
    wch = d_in // n_blk
    extra = 16 * (piece // CB)
    keep = panel * piece * n_blk * 2 <= 16 * 2**20
    sem = pltpu.SemaphoreType.DMA
    anywhere = pl.BlockSpec(memory_space=pl.ANY)
    shapes = (
        jax.ShapeDtypeStruct((piece, hid), BF16),
        jax.ShapeDtypeStruct((piece, d_in), BF16),
        jax.ShapeDtypeStruct((d_in, hid), F32),
        jax.ShapeDtypeStruct((1, hid), F32),
    )
    slots = n_blk if keep else 1
    hbm = pl.BlockSpec(memory_space=pltpu.HBM)
    results = pl.pallas_call(
        functools.partial(kernel, n_blk, n_rep, keep),
        out_shape=shapes,
        in_specs=[hbm] * 7,
        out_specs=(pl.BlockSpec(memory_space=pltpu.VMEM),) * 4,
        scratch_shapes=[
            pltpu.VMEM((piece, d_in), BF16),
            pltpu.VMEM(edge_rows.shape, jnp.int32),
            pltpu.VMEM(edge_cols.shape, jnp.int32),
            pltpu.VMEM((d_in, hid), BF16),
            pltpu.VMEM((1, hid), F32),
            pltpu.VMEM((panel // CB, CB), jnp.int32),
            pltpu.VMEM((n_blk, piece, d_in), BF16),
            pltpu.VMEM((slots, panel, piece), BF16),
            pltpu.VMEM((8 if keep else panel, d_in + CB), F32),
            pltpu.VMEM((n_rep, piece + extra, d_in), BF16),
            pltpu.VMEM((n_rep, piece + extra, d_in), BF16),
            pltpu.VMEM((piece, hid), BF16),
            pltpu.VMEM((n_rep, d_in, piece), BF16),
            pltpu.VMEM((n_blk, d_in, piece), F32),
            pltpu.VMEM((n_blk, d_in, piece), BF16),
            pltpu.VMEM((n_blk, d_in, piece), BF16),
            pltpu.VMEM((n_blk, wch + 8, hid), F32),
            pltpu.VMEM((n_blk, wch + 8, hid), F32),
            pltpu.VMEM((wch + 8, hid), F32),
            pltpu.VMEM((n_rep, wch + 8, hid), F32),
            pltpu.VMEM((wch, hid), F32),
            pltpu.VMEM((n_blk, wch, hid), F32),
            sem((n_blk,)), sem((n_blk,)),
            sem((n_rep,)), sem((n_rep,)),
            sem((n_rep,)), sem((n_rep,)),
            sem((n_blk,)), sem((n_blk,)),
            sem((n_blk,)), sem((n_blk,)),
            sem((n_rep,)), sem((n_rep,)),
            sem((n_blk,)), sem((n_blk,)),
            sem((7,)),
        ],
        compiler_params=pltpu.CompilerParams(
            collective_id=0, has_side_effects=True, vmem_limit_bytes=VMEM
        ),
    )(
        *[pltpu.with_memory_space_constraint(x, pltpu.HBM) for x in (
            features, edge_rows, edge_cols, weight, bias.reshape(1, hid),
            train_mask.reshape(panel // CB, CB), upstream,
        )]
    )
    act, gf, gw, gb = pl.pallas_call(
        write_out,
        out_shape=shapes,
        in_specs=[anywhere] * 4,
        out_specs=(hbm,) * 4,
        scratch_shapes=[sem((4,))],
        compiler_params=pltpu.CompilerParams(vmem_limit_bytes=VMEM),
    )(*results)
    return act, gf, gw, gb.reshape(hid)


def solution(mesh):
    n_blk, n_rep = mesh.shape["blk"], mesh.shape["rep"]
    return jax.shard_map(
        functools.partial(on_device, n_blk, n_rep),
        mesh=mesh,
        in_specs=(
            P(("blk", "rep"), None),
            P("blk", None, "rep", None),
            P("blk", None, "rep", None),
            P(),
            P(),
            P("blk", None),
            P("blk"),
        ),
        out_specs=(P(("blk", "rep"), None), P(("blk", "rep"), None), P(), P()),
        check_vma=False,
    )
```

```python
import functools

import jax
import jax.numpy as jnp
from jax import lax
from jax.experimental import pallas as pl
from jax.experimental.pallas import tpu as pltpu
from jax.sharding import PartitionSpec as P

CB = 128
VMEM = 48 * 2**20
F32 = jnp.float32
BF16 = jnp.bfloat16
MESH = pl.DeviceIdType.MESH
NT = (((1,), (1,)), ((), ()))


def column(row):
    return jnp.broadcast_to(row, (CB, CB)).T


def partner(me, k, count):
    other, bit = 0, 1
    while bit < count:
        other += lax.rem(lax.div(me, bit) + (k // bit) % 2, 2) * bit
        bit *= 2
    return other


def one_hot(index, count):
    length = index.shape[-1]
    spot = lax.broadcasted_iota(jnp.int32, (count, length), 0)
    return jnp.where(spot == index, 1.0, 0.0).astype(BF16)


def kernel(
    n_blk, n_rep, keep,
    feat_hbm, rows_hbm, cols_hbm, weight_hbm, bias_hbm, mask_hbm, up_hbm,
    act_ref, gf_ref, gw_ref, gb_ref,
    feat_ref, rows_ref, cols_ref, weight_ref, bias_ref, mask_ref,
    wideh, lowh, fbuf, amat, acc, psend, precv, upbuf, backs, oacc, gsend, grecv,
    w1s, w1r, w2s, w2r, w3s, w3r,
    f_ss, f_rs, p_ss, p_rs, b_ss, b_rs, g_ss, g_rs, w1_ss, w1_rs, w2_ss, w2_rs, w3_ss, w3_rs, in_sem,
):
    b = lax.axis_index("blk")
    z = lax.axis_index("rep")
    piece, d_in = feat_ref.shape
    panel = piece * n_rep
    hid = weight_ref.shape[1]
    chunks = piece // CB
    wch = d_in // n_blk

    def blk_at(k):
        return partner(b, k, n_blk)

    def rep_at(j):
        return partner(z, j, n_rep)

    def send(src, dst, ss, rs, i, **where):
        copy = pltpu.make_async_remote_copy(
            src_ref=src, dst_ref=dst, send_sem=ss.at[i], recv_sem=rs.at[i],
            device_id=where, device_id_type=MESH,
        )
        copy.start()
        return copy

    up_src = up_hbm.at[pl.ds(pl.multiple_of(z * piece, piece), piece)]
    loads = [
        pltpu.make_async_copy(src, dst, in_sem.at[i])
        for i, (src, dst) in enumerate((
            (feat_hbm, feat_ref), (rows_hbm, rows_ref), (cols_hbm, cols_ref),
            (weight_hbm, weight_ref), (bias_hbm, bias_ref), (mask_hbm, mask_ref), (up_src, upbuf),
        ))
    ]
    for load in loads:
        load.start()
    barrier = pltpu.get_barrier_semaphore()
    for k in range(1, n_blk):
        pl.semaphore_signal(barrier, inc=1, device_id={"blk": blk_at(k)}, device_id_type=MESH)
    for j in range(1, n_rep):
        pl.semaphore_signal(barrier, inc=1, device_id={"rep": rep_at(j)}, device_id_type=MESH)
    pl.semaphore_wait(barrier, n_blk + n_rep - 2)

    sent = []
    even = list(range(n_blk - 2, 0, -2))
    f_copies = {
        k: send(feat_hbm, fbuf.at[b], f_ss, f_rs, k, blk=blk_at(k)) for k in even + [1]
    }

    def hand_on():
        for k in even:
            f_copies[k].wait_recv()
            slot = fbuf.at[blk_at(k)]
            f_copies[k + 1] = send(slot, slot, f_ss, f_rs, k + 1, blk=blk_at(1))

    def all_here():
        for k in range(1, n_blk, 2):
            f_copies[k].wait_recv()

    for load in loads[0:3]:
        load.wait()
    fbuf[b] = feat_ref[...]

    def prepare(q, slot):
        for c in range(chunks):
            rows = rows_ref[0, q, pl.ds(c, 1), :]
            cols = cols_ref[0, q, pl.ds(c, 1), :]
            wideh[slot, c] = one_hot(cols + (rows & CB), 2 * CB)
            lowh[slot, c] = one_hot(rows & (CB - 1), CB)

    def build(q, slot, pairs):
        for c in range(chunks):
            rows = rows_ref[0, q, pl.ds(c, 1), :]
            low_hot = lowh[slot, c]
            pair_of = jnp.broadcast_to(rows >> 8, (16, rows.shape[-1]))
            parts = []
            for pair in pairs:
                picked = jnp.where(pair_of == pair, 1.0, 0.0).astype(BF16)
                parts.append(low_hot * jnp.concatenate([picked] * (CB // 16), axis=0))
            made = lax.dot_general(
                jnp.concatenate(parts, axis=0), wideh[slot, c], NT, preferred_element_type=F32
            ).astype(BF16)
            for i, pair in enumerate(pairs):
                for side in range(2):
                    at = pl.ds(pl.multiple_of((pair * 2 + side) * CB, CB), CB)
                    amat[slot, at, c * CB:(c + 1) * CB] = made[
                        i * CB:(i + 1) * CB, side * CB:(side + 1) * CB
                    ]

    def pairs_of(j):
        return [rep_at(j) * (chunks // 2) + p for p in range(chunks // 2)]

    every = list(range(panel // (2 * CB)))

    def with_ones(q):
        return jnp.concatenate([fbuf[q], jnp.ones((piece, CB), BF16)], axis=1)

    def pack(total, slot, more=None):
        part = total[:, :d_in].astype(BF16)
        if more is not None:
            part = (part.astype(F32) + more[0:piece].astype(F32)).astype(BF16)
        psend[slot, 0:piece, :] = part
        counts = total[:, d_in:]
        tall = jnp.concatenate(
            [counts[i * CB:(i + 1) * CB].T[0:16] for i in range(chunks)], axis=0
        )
        if more is not None:
            extra = more[piece:].astype(F32)
            pairs = [
                extra[16 * i:16 * i + 8] + extra[16 * i + 8:16 * i + 16] for i in range(chunks)
            ]
            tall = tall + jnp.concatenate([x for pair in pairs for x in (pair, pair)], axis=0)
        top = tall.astype(BF16).astype(F32)
        line = lax.broadcasted_iota(jnp.int32, tall.shape, 0)
        psend[slot, piece:, :] = jnp.where(line % 16 < 8, top, tall - top).astype(BF16)

    odd_rep = list(range(n_rep - 1, 1, -2))
    even_rep = list(range(n_rep - 2, 0, -2))
    p_copies = {}

    def piece_of(j):
        return pl.ds(pl.multiple_of(rep_at(j) * piece, piece), piece)

    def push(total, j):
        if j in even_rep:
            p_copies[j + 1].wait_recv()
            pack(total, j, precv[j + 1])
        else:
            pack(total, j)
        if j > 0:
            to = rep_at(1 if j in odd_rep else j)
            p_copies[j] = send(psend.at[j], precv.at[j], p_ss, p_rs, j, rep=to)

    blank = jnp.zeros((piece, d_in + CB), F32)
    if keep:
        first = odd_rep + even_rep
        rest = [1, 0]

        def first_build(q, carry):
            prepare(q, q)
            build(q, q, [p for j in first for p in pairs_of(j)])
            return carry

        def rest_build(q, carry):
            build(q, q, [p for j in rest for p in pairs_of(j)])
            return carry

        def part_sum(j):
            def part_step(q, total):
                return total + jnp.dot(
                    amat[q, piece_of(j), :], with_ones(q), preferred_element_type=F32
                )
            return lax.fori_loop(0, n_blk, part_step, blank, unroll=4)

        half = n_blk // 2
        lax.fori_loop(0, half, first_build, 0, unroll=2)
        hand_on()
        lax.fori_loop(half, n_blk, first_build, 0, unroll=2)
        all_here()
        for j in odd_rep:
            push(part_sum(j), j)
        held = [(part_sum(j), j) for j in even_rep]
        lax.fori_loop(0, n_blk, rest_build, 0, unroll=2)
        push(part_sum(1), 1)
        for total, j in held:
            push(total, j)
        push(part_sum(0), 0)
    else:
        hand_on()
        all_here()
        acc[...] = jnp.zeros_like(acc)

        def whole_step(q, carry):
            prepare(q, 0)
            build(q, 0, every)
            acc[...] += jnp.dot(amat[0], with_ones(q), preferred_element_type=F32)
            return carry
        lax.fori_loop(0, n_blk, whole_step, 0)
        for j in odd_rep + even_rep + [1, 0]:
            push(acc[piece_of(j), :], j)
    sent += list(f_copies.values()) + list(p_copies.values())

    for load in loads[3:]:
        load.wait()
    masked = []
    for h in range(chunks):
        mask = column(mask_ref[pl.ds(z * chunks + h, 1), :].astype(F32))
        mask = jnp.concatenate([mask] * (hid // CB), axis=1)
        masked.append(upbuf[h * CB:(h + 1) * CB, :].astype(F32) * mask)
    for j in even_rep + [1]:
        p_copies[j].wait_recv()
    b_copies = {}
    mixed, grad_pre = [], []
    for h in range(chunks):
        at = slice(h * CB, (h + 1) * CB)
        tail_at = slice(piece + 16 * h, piece + 16 * (h + 1))
        gathered = psend[0, at, :].astype(F32)
        tail = psend[0, tail_at, :].astype(F32)
        for j in even_rep + [1]:
            gathered = gathered + precv[j, at, :].astype(F32)
            tail = tail + precv[j, tail_at, :].astype(F32)
        degree_row = 1.0 + tail[0:1] + tail[8:9]
        mixed_h = ((feat_ref[at, :].astype(F32) + gathered) / column(degree_row)).astype(BF16)
        pre_act = jnp.dot(mixed_h, weight_ref[...], preferred_element_type=F32) + bias_ref[...]
        gate = jax.nn.sigmoid(pre_act)
        slope = gate * (1.0 + pre_act * (1.0 - gate))
        grad_h = (masked[h] * slope).astype(BF16)
        back = lax.dot_general(weight_ref[...], grad_h, NT, preferred_element_type=F32)
        backs[0, h] = (back / degree_row).astype(BF16)
        for j in even_rep + [1]:
            b_copies[j, h] = send(
                backs.at[0, h], backs.at[j, h], b_ss, b_rs, j * chunks + h, rep=rep_at(j)
            )
        act_ref[at, :] = (pre_act * gate).astype(BF16)
        mixed.append(mixed_h)
        grad_pre.append(grad_h)

    def relay(h):
        for j in even_rep:
            b_copies[j, h].wait_recv()
            slot = backs.at[j, h]
            b_copies[j + 1, h] = send(
                slot, backs.at[j + 1, h], b_ss, b_rs, (j + 1) * chunks + h, rep=rep_at(1)
            )

    def back_of(j):
        return jnp.concatenate([backs[j, h] for h in range(chunks)], axis=1)

    mixed = jnp.concatenate(mixed, axis=0)
    grad_pre = jnp.concatenate(grad_pre, axis=0)
    weight_part = jnp.dot(
        mixed.astype(F32).T.astype(BF16), grad_pre, preferred_element_type=F32
    )
    bias_part = jnp.broadcast_to(
        jnp.sum(grad_pre.astype(F32), axis=0, keepdims=True), (8, hid)
    )
    for q in range(n_blk):
        w1s[q, 0:wch, :] = weight_part[q * wch:(q + 1) * wch]
        w1s[q, wch:, :] = bias_part
    w1r[b] = w1s[b]
    w1_copies = [
        send(w1s.at[blk_at(k)], w1r.at[b], w1_ss, w1_rs, k, blk=blk_at(k)) for k in range(1, n_blk)
    ]
    sent += w1_copies

    def reduce_first():
        for copy in w1_copies:
            copy.wait_recv()
        total = w1r[0]
        for q in range(1, n_blk):
            total = total + w1r[q]
        w2s[...] = total
        w2r[z] = total
        copies = [
            send(w2s, w2r.at[z], w2_ss, w2_rs, j, rep=rep_at(j)) for j in range(1, n_rep)
        ]
        return copies

    def reduce_second(copies):
        for copy in copies:
            copy.wait_recv()
        total = w2r[0]
        for q in range(1, n_rep):
            total = total + w2r[q]
        gb_ref[...] = total[wch:wch + 1]
        w3s[...] = total[0:wch]
        w3r[b] = total[0:wch]
        return {k: send(w3s, w3r.at[b], w3_ss, w3_rs, k, blk=blk_at(k)) for k in even + [1]}

    def hand_on_weights(copies):
        for k in even:
            copies[k].wait_recv()
            slot = w3r.at[blk_at(k)]
            copies[k + 1] = send(slot, slot, w3_ss, w3_rs, k + 1, blk=blk_at(1))

    last = odd_rep
    if keep:
        def add_step(j, fresh=False):
            def step(q, carry):
                got = jnp.dot(back_of(j), amat[q, piece_of(j), :], preferred_element_type=F32)
                oacc[q] = got if fresh else oacc[q] + got
                return carry
            lax.fori_loop(0, n_blk, step, 0, unroll=4)

        add_step(0, True)
        for h in range(chunks):
            b_copies[1, h].wait_recv()
        relay(0)
        add_step(1)
        for h in range(1, chunks):
            relay(h)
        for j in even_rep:
            add_step(j)
        w2_copies = reduce_first()
        for j in last:
            for h in range(chunks):
                b_copies[j, h].wait_recv()
    else:
        for h in range(chunks):
            relay(h)
        for j in last + [1]:
            for h in range(chunks):
                b_copies[j, h].wait_recv()
        w2_copies = reduce_first()

        def back_step(q, carry):
            prepare(q, 0)
            build(q, 0, every)
            total = jnp.zeros((d_in, piece), F32)
            for j in range(n_rep):
                total = total + jnp.dot(
                    back_of(j), amat[0, piece_of(j), :], preferred_element_type=F32
                )
            oacc[q] = total
            return carry
        lax.fori_loop(0, n_blk, back_step, 0)

    def source_sum(k):
        q = blk_at(k)
        total = oacc[q]
        if keep:
            for j in last:
                total = total + jnp.dot(
                    back_of(j), amat[q, piece_of(j), :], preferred_element_type=F32
                )
        return total

    g_copies = {}
    for k in list(range(n_blk - 1, 0, -2)):
        gsend[k] = source_sum(k).astype(BF16)
        g_copies[k] = send(gsend.at[k], grecv.at[k], g_ss, g_rs, k, blk=blk_at(1))
    w3_copies = reduce_second(w2_copies)
    for k in even:
        total = source_sum(k)
        g_copies[k + 1].wait_recv()
        gsend[k] = (total + grecv[k + 1].astype(F32)).astype(BF16)
        g_copies[k] = send(gsend.at[k], grecv.at[k], g_ss, g_rs, k, blk=blk_at(k))
    result = source_sum(0) + back_of(0).astype(F32)
    hand_on_weights(w3_copies)
    sent += list(b_copies.values()) + list(g_copies.values()) + w2_copies + list(w3_copies.values())
    for k in [1] + list(range(2, n_blk, 2)):
        g_copies[k].wait_recv()
        result = result + grecv[k].astype(F32)
    gf_ref[...] = result.T.astype(BF16)
    for k in range(1, n_blk, 2):
        w3_copies[k].wait_recv()
    for q in range(n_blk):
        gw_ref[q * wch:(q + 1) * wch, :] = w3r[q]
    for copy in sent:
        copy.wait_send()


def write_out(*refs):
    sems = refs[-1]
    count = (len(refs) - 1) // 2
    copies = [pltpu.make_async_copy(refs[i], refs[count + i], sems.at[i]) for i in range(count)]
    for copy in copies:
        copy.start()
    for copy in copies:
        copy.wait()


def on_device(n_blk, n_rep, features, edge_rows, edge_cols, weight, bias, upstream, train_mask):
    piece, d_in = features.shape
    panel = upstream.shape[0]
    hid = weight.shape[1]
    wch = d_in // n_blk
    extra = 16 * (piece // CB)
    keep = panel * piece * n_blk * 2 <= 16 * 2**20
    sem = pltpu.SemaphoreType.DMA
    anywhere = pl.BlockSpec(memory_space=pl.ANY)
    shapes = (
        jax.ShapeDtypeStruct((piece, hid), BF16),
        jax.ShapeDtypeStruct((piece, d_in), BF16),
        jax.ShapeDtypeStruct((d_in, hid), F32),
        jax.ShapeDtypeStruct((1, hid), F32),
    )
    slots = n_blk if keep else 1
    chunks, length = edge_rows.shape[2:]
    hbm = pl.BlockSpec(memory_space=pltpu.HBM)
    results = pl.pallas_call(
        functools.partial(kernel, n_blk, n_rep, keep),
        out_shape=shapes,
        in_specs=[hbm] * 7,
        out_specs=(pl.BlockSpec(memory_space=pltpu.VMEM),) * 4,
        scratch_shapes=[
            pltpu.VMEM((piece, d_in), BF16),
            pltpu.VMEM(edge_rows.shape, jnp.int32),
            pltpu.VMEM(edge_cols.shape, jnp.int32),
            pltpu.VMEM((d_in, hid), BF16),
            pltpu.VMEM((1, hid), F32),
            pltpu.VMEM((panel // CB, CB), jnp.int32),
            pltpu.VMEM((slots, chunks, 2 * CB, length), BF16),
            pltpu.VMEM((slots, chunks, CB, length), BF16),
            pltpu.VMEM((n_blk, piece, d_in), BF16),
            pltpu.VMEM((slots, panel, piece), BF16),
            pltpu.VMEM((8 if keep else panel, d_in + CB), F32),
            pltpu.VMEM((n_rep, piece + extra, d_in), BF16),
            pltpu.VMEM((n_rep, piece + extra, d_in), BF16),
            pltpu.VMEM((piece, hid), BF16),
            pltpu.VMEM((n_rep, chunks, d_in, CB), BF16),
            pltpu.VMEM((n_blk, d_in, piece), F32),
            pltpu.VMEM((n_blk, d_in, piece), BF16),
            pltpu.VMEM((n_blk, d_in, piece), BF16),
            pltpu.VMEM((n_blk, wch + 8, hid), F32),
            pltpu.VMEM((n_blk, wch + 8, hid), F32),
            pltpu.VMEM((wch + 8, hid), F32),
            pltpu.VMEM((n_rep, wch + 8, hid), F32),
            pltpu.VMEM((wch, hid), F32),
            pltpu.VMEM((n_blk, wch, hid), F32),
            sem((n_blk,)), sem((n_blk,)),
            sem((n_rep,)), sem((n_rep,)),
            sem((n_rep * chunks,)), sem((n_rep * chunks,)),
            sem((n_blk,)), sem((n_blk,)),
            sem((n_blk,)), sem((n_blk,)),
            sem((n_rep,)), sem((n_rep,)),
            sem((n_blk,)), sem((n_blk,)),
            sem((7,)),
        ],
        compiler_params=pltpu.CompilerParams(
            collective_id=0, has_side_effects=True, vmem_limit_bytes=VMEM
        ),
    )(
        *[pltpu.with_memory_space_constraint(x, pltpu.HBM) for x in (
            features, edge_rows, edge_cols, weight, bias.reshape(1, hid),
            train_mask.reshape(panel // CB, CB), upstream,
        )]
    )
    act, gf, gw, gb = pl.pallas_call(
        write_out,
        out_shape=shapes,
        in_specs=[anywhere] * 4,
        out_specs=(hbm,) * 4,
        scratch_shapes=[sem((4,))],
        compiler_params=pltpu.CompilerParams(vmem_limit_bytes=VMEM),
    )(*results)
    return act, gf, gw, gb.reshape(hid)


def solution(mesh):
    n_blk, n_rep = mesh.shape["blk"], mesh.shape["rep"]
    return jax.shard_map(
        functools.partial(on_device, n_blk, n_rep),
        mesh=mesh,
        in_specs=(
            P(("blk", "rep"), None),
            P("blk", None, "rep", None),
            P("blk", None, "rep", None),
            P(),
            P(),
            P("blk", None),
            P("blk"),
        ),
        out_specs=(P(("blk", "rep"), None), P(("blk", "rep"), None), P(), P()),
        check_vma=False,
    )
```

```python
import functools

import jax
import jax.numpy as jnp
from jax import lax
from jax.experimental import pallas as pl
from jax.experimental.pallas import tpu as pltpu
from jax.sharding import PartitionSpec as P

CB = 128
VMEM = 48 * 2**20
F32 = jnp.float32
BF16 = jnp.bfloat16
MESH = pl.DeviceIdType.MESH
NT = (((1,), (1,)), ((), ()))


def column(row):
    return jnp.broadcast_to(row, (CB, CB)).T


def partner(me, k, count):
    other, bit = 0, 1
    while bit < count:
        other += lax.rem(lax.div(me, bit) + (k // bit) % 2, 2) * bit
        bit *= 2
    return other


def one_hot(index, count):
    length = index.shape[-1]
    spot = lax.broadcasted_iota(jnp.int32, (count, length), 0)
    return jnp.where(spot == index, 1.0, 0.0).astype(BF16)


def kernel(
    n_blk, n_rep, keep,
    feat_hbm, rows_hbm, cols_hbm, weight_hbm, bias_hbm, mask_hbm, up_hbm,
    act_ref, gf_ref, gw_ref, gb_ref,
    feat_ref, rows_ref, cols_ref, weight_ref, bias_ref, mask_ref,
    wideh, lowh, fbuf, amat, acc, psend, precv, upbuf, backs, oacc, gsend, grecv,
    w1s, w1r, w2s, w2r, w3s, w3r,
    f_ss, f_rs, p_ss, p_rs, b_ss, b_rs, g_ss, g_rs, w1_ss, w1_rs, w2_ss, w2_rs, w3_ss, w3_rs, in_sem,
):
    b = lax.axis_index("blk")
    z = lax.axis_index("rep")
    piece, d_in = feat_ref.shape
    panel = piece * n_rep
    hid = weight_ref.shape[1]
    chunks = piece // CB
    wch = d_in // n_blk

    def blk_at(k):
        return partner(b, k, n_blk)

    def rep_at(j):
        return partner(z, j, n_rep)

    def send(src, dst, ss, rs, i, **where):
        copy = pltpu.make_async_remote_copy(
            src_ref=src, dst_ref=dst, send_sem=ss.at[i], recv_sem=rs.at[i],
            device_id=where, device_id_type=MESH,
        )
        copy.start()
        return copy

    up_src = up_hbm.at[pl.ds(pl.multiple_of(z * piece, piece), piece)]
    loads = [
        pltpu.make_async_copy(src, dst, in_sem.at[i])
        for i, (src, dst) in enumerate((
            (feat_hbm, feat_ref), (rows_hbm, rows_ref), (cols_hbm, cols_ref),
            (weight_hbm, weight_ref), (bias_hbm, bias_ref), (mask_hbm, mask_ref), (up_src, upbuf),
        ))
    ]
    for load in loads:
        load.start()
    barrier = pltpu.get_barrier_semaphore()
    for k in range(1, n_blk):
        pl.semaphore_signal(barrier, inc=1, device_id={"blk": blk_at(k)}, device_id_type=MESH)
    for j in range(1, n_rep):
        pl.semaphore_signal(barrier, inc=1, device_id={"rep": rep_at(j)}, device_id_type=MESH)
    pl.semaphore_wait(barrier, n_blk + n_rep - 2)

    sent = []
    even = list(range(n_blk - 2, 0, -2))
    f_copies = {
        k: send(feat_hbm, fbuf.at[b], f_ss, f_rs, k, blk=blk_at(k)) for k in range(n_blk - 1, 0, -1)
    }

    def all_here():
        for copy in f_copies.values():
            copy.wait_recv()

    for load in loads[0:3]:
        load.wait()
    fbuf[b] = feat_ref[...]

    def prepare(q, c, slot):
        rows = rows_ref[0, q, pl.ds(c, 1), :]
        cols = cols_ref[0, q, pl.ds(c, 1), :]
        wideh[slot, c] = one_hot(cols + (rows & CB), 2 * CB)
        lowh[slot, c] = one_hot(rows & (CB - 1), CB)

    def build(q, c, slot, pairs):
        rows = rows_ref[0, q, pl.ds(c, 1), :]
        low_hot = lowh[slot, c]
        pair_of = jnp.broadcast_to(rows >> 8, (16, rows.shape[-1]))
        parts = []
        for pair in pairs:
            picked = jnp.where(pair_of == pair, 1.0, 0.0).astype(BF16)
            parts.append(low_hot * jnp.concatenate([picked] * (CB // 16), axis=0))
        made = lax.dot_general(
            jnp.concatenate(parts, axis=0), wideh[slot, c], NT, preferred_element_type=F32
        ).astype(BF16)
        lanes = pl.ds(pl.multiple_of(c * CB, CB), CB)
        for i, pair in enumerate(pairs):
            for side in range(2):
                at = pl.ds(pl.multiple_of((pair * 2 + side) * CB, CB), CB)
                amat[slot, at, lanes] = made[i * CB:(i + 1) * CB, side * CB:(side + 1) * CB]

    def build_all(q):
        def step(c, carry):
            prepare(q, c, 0)
            build(q, c, 0, every)
            return carry
        lax.fori_loop(0, chunks, step, 0)

    def pairs_of(j):
        return [rep_at(j) * (chunks // 2) + p for p in range(chunks // 2)]

    every = list(range(panel // (2 * CB)))

    def with_ones(q):
        return jnp.concatenate([fbuf[q], jnp.ones((piece, CB), BF16)], axis=1)

    def pack(total, slot):
        psend[slot, 0:piece, :] = total[:, :d_in].astype(BF16)
        counts = total[:, d_in:]
        tall = jnp.concatenate(
            [counts[i * CB:(i + 1) * CB].T[0:16] for i in range(chunks)], axis=0
        )
        top = tall.astype(BF16).astype(F32)
        line = lax.broadcasted_iota(jnp.int32, tall.shape, 0)
        psend[slot, piece:, :] = jnp.where(line % 16 < 8, top, tall - top).astype(BF16)

    odd_rep = list(range(n_rep - 1, 1, -2))
    even_rep = list(range(n_rep - 2, 0, -2))
    p_copies = {}

    def piece_of(j):
        return pl.ds(pl.multiple_of(rep_at(j) * piece, piece), piece)

    def push(total, j):
        pack(total, j)
        if j > 0:
            p_copies[j] = send(psend.at[j], precv.at[j], p_ss, p_rs, j, rep=rep_at(j))

    blank = jnp.zeros((piece, d_in + CB), F32)
    if keep:
        first = even_rep + odd_rep
        rest = [1, 0]

        def first_build(i, carry):
            q, c = lax.div(i, chunks), lax.rem(i, chunks)
            prepare(q, c, q)
            build(q, c, q, [p for j in first for p in pairs_of(j)])
            return carry

        def rest_build(i, carry):
            q, c = lax.div(i, chunks), lax.rem(i, chunks)
            build(q, c, q, [p for j in rest for p in pairs_of(j)])
            return carry

        def part_sum(j):
            def part_step(q, total):
                return total + jnp.dot(
                    amat[q, piece_of(j), :], with_ones(q), preferred_element_type=F32
                )
            return lax.fori_loop(0, n_blk, part_step, blank)

        lax.fori_loop(0, n_blk * chunks, first_build, 0)
        all_here()
        for j in first:
            push(part_sum(j), j)
        lax.fori_loop(0, n_blk * chunks, rest_build, 0)
        for j in rest:
            push(part_sum(j), j)
    else:
        all_here()
        acc[...] = jnp.zeros_like(acc)

        def whole_step(q, carry):
            build_all(q)
            acc[...] += jnp.dot(amat[0], with_ones(q), preferred_element_type=F32)
            return carry
        lax.fori_loop(0, n_blk, whole_step, 0)
        for j in odd_rep + even_rep + [1, 0]:
            push(acc[piece_of(j), :], j)
    sent += list(f_copies.values()) + list(p_copies.values())

    for load in loads[3:]:
        load.wait()
    masked = []
    for h in range(chunks):
        mask = column(mask_ref[pl.ds(z * chunks + h, 1), :].astype(F32))
        mask = jnp.concatenate([mask] * (hid // CB), axis=1)
        masked.append(upbuf[h * CB:(h + 1) * CB, :].astype(F32) * mask)
    others = even_rep + odd_rep + [1]
    for j in others:
        p_copies[j].wait_recv()
    b_copies = {}
    mixed, grad_pre, active = [], [], []
    for h in range(chunks):
        at = slice(h * CB, (h + 1) * CB)
        tail_at = slice(piece + 16 * h, piece + 16 * (h + 1))
        gathered = psend[0, at, :].astype(F32)
        tail = psend[0, tail_at, :].astype(F32)
        for j in others:
            gathered = gathered + precv[j, at, :].astype(F32)
            tail = tail + precv[j, tail_at, :].astype(F32)
        degree_row = 1.0 + tail[0:1] + tail[8:9]
        mixed_h = ((feat_ref[at, :].astype(F32) + gathered) / column(degree_row)).astype(BF16)
        pre_act = jnp.dot(mixed_h, weight_ref[...], preferred_element_type=F32) + bias_ref[...]
        gate = jax.nn.sigmoid(pre_act)
        slope = gate * (1.0 + pre_act * (1.0 - gate))
        grad_h = (masked[h] * slope).astype(BF16)
        back = lax.dot_general(weight_ref[...], grad_h, NT, preferred_element_type=F32)
        backs[0, h] = (back / degree_row).astype(BF16)
        active.append(pre_act * gate)
        mixed.append(mixed_h)
        grad_pre.append(grad_h)

    for j in others:
        b_copies[j] = send(backs.at[0], backs.at[j], b_ss, b_rs, j, rep=rep_at(j))
    for h in range(chunks):
        act_ref[h * CB:(h + 1) * CB, :] = active[h].astype(BF16)

    def back_of(j):
        return jnp.concatenate([backs[j, h] for h in range(chunks)], axis=1)

    mixed = jnp.concatenate(mixed, axis=0)
    grad_pre = jnp.concatenate(grad_pre, axis=0)
    weight_part = jnp.dot(
        mixed.astype(F32).T.astype(BF16), grad_pre, preferred_element_type=F32
    )
    bias_part = jnp.broadcast_to(
        jnp.sum(grad_pre.astype(F32), axis=0, keepdims=True), (8, hid)
    )
    for q in range(n_blk):
        w1s[q, 0:wch, :] = weight_part[q * wch:(q + 1) * wch]
        w1s[q, wch:, :] = bias_part
    w1r[b] = w1s[b]
    w1_copies = [
        send(w1s.at[blk_at(k)], w1r.at[b], w1_ss, w1_rs, k, blk=blk_at(k)) for k in range(1, n_blk)
    ]
    sent += w1_copies

    def reduce_first():
        for copy in w1_copies:
            copy.wait_recv()
        total = w1r[0]
        for q in range(1, n_blk):
            total = total + w1r[q]
        w2s[...] = total
        w2r[z] = total
        copies = [
            send(w2s, w2r.at[z], w2_ss, w2_rs, j, rep=rep_at(j)) for j in range(1, n_rep)
        ]
        return copies

    def reduce_second(copies):
        for copy in copies:
            copy.wait_recv()
        total = w2r[0]
        for q in range(1, n_rep):
            total = total + w2r[q]
        gb_ref[...] = total[wch:wch + 1]
        w3s[...] = total[0:wch]
        w3r[b] = total[0:wch]
        return {
            k: send(w3s, w3r.at[b], w3_ss, w3_rs, k, blk=blk_at(k)) for k in range(1, n_blk)
        }

    if keep:
        def add_step(j, fresh=False):
            def step(q, carry):
                got = jnp.dot(back_of(j), amat[q, piece_of(j), :], preferred_element_type=F32)
                oacc[q] = got if fresh else oacc[q] + got
                return carry
            lax.fori_loop(0, n_blk, step, 0)

        add_step(0, True)
        turns = [1] + even_rep + odd_rep
        for j in turns[:-1]:
            b_copies[j].wait_recv()
            add_step(j)
        w2_copies = reduce_first()
        b_copies[turns[-1]].wait_recv()
        add_step(turns[-1])
    else:
        for j in others:
            b_copies[j].wait_recv()
        w2_copies = reduce_first()

        def back_step(q, carry):
            build_all(q)
            total = jnp.zeros((d_in, piece), F32)
            for j in range(n_rep):
                total = total + jnp.dot(
                    back_of(j), amat[0, piece_of(j), :], preferred_element_type=F32
                )
            oacc[q] = total
            return carry
        lax.fori_loop(0, n_blk, back_step, 0)

    def source_sum(k):
        return oacc[blk_at(k)]

    g_copies = {}
    for k in list(range(n_blk - 1, 0, -2)):
        gsend[k] = source_sum(k).astype(BF16)
        g_copies[k] = send(gsend.at[k], grecv.at[k], g_ss, g_rs, k, blk=blk_at(1))
    for k in even:
        total = source_sum(k)
        g_copies[k + 1].wait_recv()
        gsend[k] = (total + grecv[k + 1].astype(F32)).astype(BF16)
        g_copies[k] = send(gsend.at[k], grecv.at[k], g_ss, g_rs, k, blk=blk_at(k))
    w3_copies = reduce_second(w2_copies)
    result = source_sum(0) + back_of(0).astype(F32)
    sent += list(b_copies.values()) + list(g_copies.values()) + w2_copies + list(w3_copies.values())
    for k in [1] + list(range(2, n_blk, 2)):
        g_copies[k].wait_recv()
        result = result + grecv[k].astype(F32)
    gf_ref[...] = result.T.astype(BF16)
    for copy in w3_copies.values():
        copy.wait_recv()
    for q in range(n_blk):
        gw_ref[q * wch:(q + 1) * wch, :] = w3r[q]
    for copy in sent:
        copy.wait_send()


def write_out(*refs):
    sems = refs[-1]
    count = (len(refs) - 1) // 2
    copies = [pltpu.make_async_copy(refs[i], refs[count + i], sems.at[i]) for i in range(count)]
    for copy in copies:
        copy.start()
    for copy in copies:
        copy.wait()


def on_device(n_blk, n_rep, features, edge_rows, edge_cols, weight, bias, upstream, train_mask):
    piece, d_in = features.shape
    panel = upstream.shape[0]
    hid = weight.shape[1]
    wch = d_in // n_blk
    extra = 16 * (piece // CB)
    keep = panel * piece * n_blk * 2 <= 16 * 2**20
    sem = pltpu.SemaphoreType.DMA
    anywhere = pl.BlockSpec(memory_space=pl.ANY)
    shapes = (
        jax.ShapeDtypeStruct((piece, hid), BF16),
        jax.ShapeDtypeStruct((piece, d_in), BF16),
        jax.ShapeDtypeStruct((d_in, hid), F32),
        jax.ShapeDtypeStruct((1, hid), F32),
    )
    slots = n_blk if keep else 1
    chunks, length = edge_rows.shape[2:]
    hbm = pl.BlockSpec(memory_space=pltpu.HBM)
    results = pl.pallas_call(
        functools.partial(kernel, n_blk, n_rep, keep),
        out_shape=shapes,
        in_specs=[hbm] * 7,
        out_specs=(pl.BlockSpec(memory_space=pltpu.VMEM),) * 4,
        scratch_shapes=[
            pltpu.VMEM((piece, d_in), BF16),
            pltpu.VMEM(edge_rows.shape, jnp.int32),
            pltpu.VMEM(edge_cols.shape, jnp.int32),
            pltpu.VMEM((d_in, hid), BF16),
            pltpu.VMEM((1, hid), F32),
            pltpu.VMEM((panel // CB, CB), jnp.int32),
            pltpu.VMEM((slots, chunks, 2 * CB, length), BF16),
            pltpu.VMEM((slots, chunks, CB, length), BF16),
            pltpu.VMEM((n_blk, piece, d_in), BF16),
            pltpu.VMEM((slots, panel, piece), BF16),
            pltpu.VMEM((8 if keep else panel, d_in + CB), F32),
            pltpu.VMEM((n_rep, piece + extra, d_in), BF16),
            pltpu.VMEM((n_rep, piece + extra, d_in), BF16),
            pltpu.VMEM((piece, hid), BF16),
            pltpu.VMEM((n_rep, chunks, d_in, CB), BF16),
            pltpu.VMEM((n_blk, d_in, piece), F32),
            pltpu.VMEM((n_blk, d_in, piece), BF16),
            pltpu.VMEM((n_blk, d_in, piece), BF16),
            pltpu.VMEM((n_blk, wch + 8, hid), F32),
            pltpu.VMEM((n_blk, wch + 8, hid), F32),
            pltpu.VMEM((wch + 8, hid), F32),
            pltpu.VMEM((n_rep, wch + 8, hid), F32),
            pltpu.VMEM((wch, hid), F32),
            pltpu.VMEM((n_blk, wch, hid), F32),
            sem((n_blk,)), sem((n_blk,)),
            sem((n_rep,)), sem((n_rep,)),
            sem((n_rep * chunks,)), sem((n_rep * chunks,)),
            sem((n_blk,)), sem((n_blk,)),
            sem((n_blk,)), sem((n_blk,)),
            sem((n_rep,)), sem((n_rep,)),
            sem((n_blk,)), sem((n_blk,)),
            sem((7,)),
        ],
        compiler_params=pltpu.CompilerParams(
            collective_id=0, has_side_effects=True, vmem_limit_bytes=VMEM
        ),
    )(
        *[pltpu.with_memory_space_constraint(x, pltpu.HBM) for x in (
            features, edge_rows, edge_cols, weight, bias.reshape(1, hid),
            train_mask.reshape(panel // CB, CB), upstream,
        )]
    )
    act, gf, gw, gb = pl.pallas_call(
        write_out,
        out_shape=shapes,
        in_specs=[anywhere] * 4,
        out_specs=(hbm,) * 4,
        scratch_shapes=[sem((4,))],
        compiler_params=pltpu.CompilerParams(vmem_limit_bytes=VMEM),
    )(*results)
    return act, gf, gw, gb.reshape(hid)


def solution(mesh):
    n_blk, n_rep = mesh.shape["blk"], mesh.shape["rep"]
    return jax.shard_map(
        functools.partial(on_device, n_blk, n_rep),
        mesh=mesh,
        in_specs=(
            P(("blk", "rep"), None),
            P("blk", None, "rep", None),
            P("blk", None, "rep", None),
            P(),
            P(),
            P("blk", None),
            P("blk"),
        ),
        out_specs=(P(("blk", "rep"), None), P(("blk", "rep"), None), P(), P()),
        check_vma=False,
    )
```

```python
import functools

import jax
import jax.numpy as jnp
from jax import lax
from jax.experimental import pallas as pl
from jax.experimental.pallas import tpu as pltpu
from jax.sharding import PartitionSpec as P

CB = 128
VMEM = 48 * 2**20
F32 = jnp.float32
BF16 = jnp.bfloat16
MESH = pl.DeviceIdType.MESH
NT = (((1,), (1,)), ((), ()))


def column(row):
    return jnp.broadcast_to(row, (CB, CB)).T


def partner(me, k, count):
    other, bit = 0, 1
    while bit < count:
        other += lax.rem(lax.div(me, bit) + (k // bit) % 2, 2) * bit
        bit *= 2
    return other


def one_hot(index, count):
    length = index.shape[-1]
    spot = lax.broadcasted_iota(jnp.int32, (count, length), 0)
    return jnp.where(spot == index, 1.0, 0.0).astype(BF16)


def kernel(
    n_blk, n_rep, keep,
    feat_hbm, rows_hbm, cols_hbm, weight_hbm, bias_hbm, mask_hbm, up_hbm,
    act_ref, gf_ref, gw_ref, gb_ref,
    feat_ref, rows_ref, cols_ref, weight_ref, bias_ref, mask_ref,
    fbuf, amat, acc, psend, precv, upbuf, backs, oacc, gsend, grecv,
    w1s, w1r, w2s, w2r, w3s, w3r,
    f_ss, f_rs, p_ss, p_rs, b_ss, b_rs, g_ss, g_rs, w1_ss, w1_rs, w2_ss, w2_rs, w3_ss, w3_rs, in_sem,
):
    b = lax.axis_index("blk")
    z = lax.axis_index("rep")
    piece, d_in = feat_ref.shape
    panel = piece * n_rep
    hid = weight_ref.shape[1]
    chunks = piece // CB
    wch = d_in // n_blk

    def blk_at(k):
        return partner(b, k, n_blk)

    def rep_at(j):
        return partner(z, j, n_rep)

    def send(src, dst, ss, rs, i, **where):
        copy = pltpu.make_async_remote_copy(
            src_ref=src, dst_ref=dst, send_sem=ss.at[i], recv_sem=rs.at[i],
            device_id=where, device_id_type=MESH,
        )
        copy.start()
        return copy

    up_src = up_hbm.at[pl.ds(pl.multiple_of(z * piece, piece), piece)]
    loads = [
        pltpu.make_async_copy(src, dst, in_sem.at[i])
        for i, (src, dst) in enumerate((
            (feat_hbm, feat_ref), (rows_hbm, rows_ref), (cols_hbm, cols_ref),
            (weight_hbm, weight_ref), (bias_hbm, bias_ref), (mask_hbm, mask_ref), (up_src, upbuf),
        ))
    ]
    for load in loads:
        load.start()
    barrier = pltpu.get_barrier_semaphore()
    for k in range(1, n_blk):
        pl.semaphore_signal(barrier, inc=1, device_id={"blk": blk_at(k)}, device_id_type=MESH)
    for j in range(1, n_rep):
        pl.semaphore_signal(barrier, inc=1, device_id={"rep": rep_at(j)}, device_id_type=MESH)
    loads[0].wait()
    pl.semaphore_wait(barrier, n_blk + n_rep - 2)

    sent = []
    even = list(range(n_blk - 2, 0, -2))
    f_copies = {
        k: send(feat_ref, fbuf.at[b], f_ss, f_rs, k, blk=blk_at(k)) for k in even + [1]
    }

    def hand_on():
        for k in even:
            f_copies[k].wait_recv()
            slot = fbuf.at[blk_at(k)]
            f_copies[k + 1] = send(slot, slot, f_ss, f_rs, k + 1, blk=blk_at(1))

    def all_here():
        for k in range(1, n_blk, 2):
            f_copies[k].wait_recv()

    fbuf[b] = feat_ref[...]
    for load in loads[1:3]:
        load.wait()

    def build(q, slot):
        for c in range(chunks):
            rows = rows_ref[0, q, pl.ds(c, 1), :]
            cols = cols_ref[0, q, pl.ds(c, 1), :]
            wide_hot = one_hot(cols + (rows & CB), 2 * CB)
            low_hot = one_hot(rows & (CB - 1), CB)
            pair = jnp.broadcast_to(rows >> 8, (16, rows.shape[-1]))
            parts = []
            for h in range(panel // (2 * CB)):
                picked = jnp.where(pair == h, 1.0, 0.0).astype(BF16)
                parts.append(low_hot * jnp.concatenate([picked] * (CB // 16), axis=0))
            made = lax.dot_general(
                jnp.concatenate(parts, axis=0), wide_hot, NT, preferred_element_type=F32
            ).astype(BF16)
            for h in range(panel // CB):
                amat[slot, h * CB:(h + 1) * CB, c * CB:(c + 1) * CB] = made[
                    (h // 2) * CB:(h // 2 + 1) * CB, (h % 2) * CB:(h % 2 + 1) * CB
                ]

    def with_ones(q):
        return jnp.concatenate([fbuf[q], jnp.ones((piece, CB), BF16)], axis=1)

    def pack(total, slot, more=None):
        part = total[:, :d_in].astype(BF16)
        if more is not None:
            part = (part.astype(F32) + more[0:piece].astype(F32)).astype(BF16)
        psend[slot, 0:piece, :] = part
        counts = total[:, d_in:]
        tall = jnp.concatenate(
            [counts[i * CB:(i + 1) * CB].T[0:16] for i in range(chunks)], axis=0
        )
        if more is not None:
            extra = more[piece:].astype(F32)
            pairs = [
                extra[16 * i:16 * i + 8] + extra[16 * i + 8:16 * i + 16] for i in range(chunks)
            ]
            tall = tall + jnp.concatenate([x for pair in pairs for x in (pair, pair)], axis=0)
        top = tall.astype(BF16).astype(F32)
        line = lax.broadcasted_iota(jnp.int32, tall.shape, 0)
        psend[slot, piece:, :] = jnp.where(line % 16 < 8, top, tall - top).astype(BF16)

    odd_rep = list(range(n_rep - 1, 1, -2))
    even_rep = list(range(n_rep - 2, 0, -2))
    order = even_rep + odd_rep + [1]
    p_copies = {}

    def piece_of(j):
        return pl.ds(pl.multiple_of(rep_at(j) * piece, piece), piece)

    def push(total, j):
        if j in even_rep:
            p_copies[j + 1].wait_recv()
            pack(total, j, precv[j + 1])
        else:
            pack(total, j)
        if j > 0:
            to = rep_at(1 if j in odd_rep else j)
            p_copies[j] = send(psend.at[j], precv.at[j], p_ss, p_rs, j, rep=to)

    blank = jnp.zeros((piece, d_in + CB), F32)
    if keep:
        def build_step(q, carry):
            build(q, q)
            return carry
        half = n_blk // 2
        lax.fori_loop(0, half, build_step, 0, unroll=4)
        hand_on()
        lax.fori_loop(half, n_blk, build_step, 0, unroll=4)
        all_here()
        for j in odd_rep + [1] + even_rep + [0]:
            def part_step(q, total, j=j):
                return total + jnp.dot(
                    amat[q, piece_of(j), :], with_ones(q), preferred_element_type=F32
                )
            push(lax.fori_loop(0, n_blk, part_step, blank, unroll=8), j)
    else:
        hand_on()
        all_here()
        acc[...] = jnp.zeros_like(acc)

        def whole_step(q, carry):
            build(q, 0)
            acc[...] += jnp.dot(amat[0], with_ones(q), preferred_element_type=F32)
            return carry
        lax.fori_loop(0, n_blk, whole_step, 0)
        for j in odd_rep + even_rep + [1, 0]:
            push(acc[piece_of(j), :], j)
    sent += list(f_copies.values()) + list(p_copies.values())

    gathered = psend[0, 0:piece, :].astype(F32)
    tail = psend[0, piece:, :].astype(F32)
    for load in loads[3:]:
        load.wait()
    for j in even_rep + [1]:
        p_copies[j].wait_recv()
        gathered = gathered + precv[j, 0:piece, :].astype(F32)
        tail = tail + precv[j, piece:, :].astype(F32)
    degree_rows = [
        1.0 + tail[16 * i:16 * i + 1] + tail[16 * i + 8:16 * i + 9] for i in range(chunks)
    ]
    degree = jnp.concatenate([column(row) for row in degree_rows], axis=0)
    mixed = ((feat_ref[...].astype(F32) + gathered) / degree).astype(BF16)
    pre_act = jnp.dot(mixed, weight_ref[...], preferred_element_type=F32) + bias_ref[...]
    gate = jax.nn.sigmoid(pre_act)
    slope = gate * (1.0 + pre_act * (1.0 - gate))
    mask = jnp.concatenate(
        [column(mask_ref[pl.ds(z * chunks + i, 1), :].astype(F32)) for i in range(chunks)], axis=0
    )
    mask = jnp.concatenate([mask] * (hid // CB), axis=1)
    grad_pre = (upbuf[...].astype(F32) * mask * slope).astype(BF16)
    back = lax.dot_general(weight_ref[...], grad_pre, NT, preferred_element_type=F32)
    backs[0] = (back / jnp.concatenate(degree_rows, axis=1)).astype(BF16)
    b_copies = {
        j: send(backs.at[0], backs.at[j], b_ss, b_rs, j, rep=rep_at(j)) for j in order
    }
    sent += list(b_copies.values())

    act_ref[...] = (pre_act * gate).astype(BF16)
    weight_part = jnp.dot(
        mixed.astype(F32).T.astype(BF16), grad_pre, preferred_element_type=F32
    )
    bias_part = jnp.broadcast_to(
        jnp.sum(grad_pre.astype(F32), axis=0, keepdims=True), (8, hid)
    )
    for q in range(n_blk):
        w1s[q, 0:wch, :] = weight_part[q * wch:(q + 1) * wch]
        w1s[q, wch:, :] = bias_part
    w1r[b] = w1s[b]
    w1_copies = [
        send(w1s.at[blk_at(k)], w1r.at[b], w1_ss, w1_rs, k, blk=blk_at(k)) for k in range(1, n_blk)
    ]
    sent += w1_copies

    def reduce_first():
        for copy in w1_copies:
            copy.wait_recv()
        total = w1r[0]
        for q in range(1, n_blk):
            total = total + w1r[q]
        w2s[...] = total
        w2r[z] = total
        copies = [
            send(w2s, w2r.at[z], w2_ss, w2_rs, j, rep=rep_at(j)) for j in range(1, n_rep)
        ]
        return copies

    def reduce_second(copies):
        for copy in copies:
            copy.wait_recv()
        total = w2r[0]
        for q in range(1, n_rep):
            total = total + w2r[q]
        gb_ref[...] = total[wch:wch + 1]
        w3s[...] = total[0:wch]
        w3r[b] = total[0:wch]
        return {k: send(w3s, w3r.at[b], w3_ss, w3_rs, k, blk=blk_at(k)) for k in even + [1]}

    def hand_on_weights(copies):
        for k in even:
            copies[k].wait_recv()
            slot = w3r.at[blk_at(k)]
            copies[k + 1] = send(slot, slot, w3_ss, w3_rs, k + 1, blk=blk_at(1))

    arrive = list(range(1, n_rep))
    if keep:
        def first_step(q, carry):
            oacc[q] = jnp.dot(backs[0], amat[q, piece_of(0), :], preferred_element_type=F32)
            return carry
        lax.fori_loop(0, n_blk, first_step, 0, unroll=8)
        for j in arrive[:-1]:
            b_copies[j].wait_recv()

            def more_step(q, carry, j=j):
                oacc[q] += jnp.dot(backs[j], amat[q, piece_of(j), :], preferred_element_type=F32)
                return carry
            lax.fori_loop(0, n_blk, more_step, 0, unroll=8)
        w2_copies = reduce_first()
        b_copies[arrive[-1]].wait_recv()
    else:
        w2_copies = reduce_first()
        for j in arrive:
            b_copies[j].wait_recv()

        def back_step(q, carry):
            build(q, 0)
            total = jnp.dot(backs[0], amat[0, piece_of(0), :], preferred_element_type=F32)
            for j in arrive:
                total = total + jnp.dot(backs[j], amat[0, piece_of(j), :], preferred_element_type=F32)
            oacc[q] = total
            return carry
        lax.fori_loop(0, n_blk, back_step, 0)

    def source_sum(k):
        q = blk_at(k)
        total = oacc[q]
        if keep:
            j = arrive[-1]
            total = total + jnp.dot(backs[j], amat[q, piece_of(j), :], preferred_element_type=F32)
        return total

    g_copies = {}
    for k in list(range(n_blk - 1, 0, -2)):
        gsend[k] = source_sum(k).astype(BF16)
        g_copies[k] = send(gsend.at[k], grecv.at[k], g_ss, g_rs, k, blk=blk_at(1))
    w3_copies = reduce_second(w2_copies)
    for k in even:
        total = source_sum(k)
        g_copies[k + 1].wait_recv()
        gsend[k] = (total + grecv[k + 1].astype(F32)).astype(BF16)
        g_copies[k] = send(gsend.at[k], grecv.at[k], g_ss, g_rs, k, blk=blk_at(k))
    result = source_sum(0) + backs[0].astype(F32)
    hand_on_weights(w3_copies)
    sent += list(g_copies.values()) + w2_copies + list(w3_copies.values())
    for k in [1] + list(range(2, n_blk, 2)):
        g_copies[k].wait_recv()
        result = result + grecv[k].astype(F32)
    gf_ref[...] = result.T.astype(BF16)
    for k in range(1, n_blk, 2):
        w3_copies[k].wait_recv()
    for q in range(n_blk):
        gw_ref[q * wch:(q + 1) * wch, :] = w3r[q]
    for copy in sent:
        copy.wait_send()


def write_out(*refs):
    sems = refs[-1]
    count = (len(refs) - 1) // 2
    copies = [pltpu.make_async_copy(refs[i], refs[count + i], sems.at[i]) for i in range(count)]
    for copy in copies:
        copy.start()
    for copy in copies:
        copy.wait()


def on_device(n_blk, n_rep, features, edge_rows, edge_cols, weight, bias, upstream, train_mask):
    piece, d_in = features.shape
    panel = upstream.shape[0]
    hid = weight.shape[1]
    wch = d_in // n_blk
    extra = 16 * (piece // CB)
    keep = panel * piece * n_blk * 2 <= 16 * 2**20
    sem = pltpu.SemaphoreType.DMA
    anywhere = pl.BlockSpec(memory_space=pl.ANY)
    shapes = (
        jax.ShapeDtypeStruct((piece, hid), BF16),
        jax.ShapeDtypeStruct((piece, d_in), BF16),
        jax.ShapeDtypeStruct((d_in, hid), F32),
        jax.ShapeDtypeStruct((1, hid), F32),
    )
    slots = n_blk if keep else 1
    hbm = pl.BlockSpec(memory_space=pltpu.HBM)
    results = pl.pallas_call(
        functools.partial(kernel, n_blk, n_rep, keep),
        out_shape=shapes,
        in_specs=[hbm] * 7,
        out_specs=(pl.BlockSpec(memory_space=pltpu.VMEM),) * 4,
        scratch_shapes=[
            pltpu.VMEM((piece, d_in), BF16),
            pltpu.VMEM(edge_rows.shape, jnp.int32),
            pltpu.VMEM(edge_cols.shape, jnp.int32),
            pltpu.VMEM((d_in, hid), BF16),
            pltpu.VMEM((1, hid), F32),
            pltpu.VMEM((panel // CB, CB), jnp.int32),
            pltpu.VMEM((n_blk, piece, d_in), BF16),
            pltpu.VMEM((slots, panel, piece), BF16),
            pltpu.VMEM((8 if keep else panel, d_in + CB), F32),
            pltpu.VMEM((n_rep, piece + extra, d_in), BF16),
            pltpu.VMEM((n_rep, piece + extra, d_in), BF16),
            pltpu.VMEM((piece, hid), BF16),
            pltpu.VMEM((n_rep, d_in, piece), BF16),
            pltpu.VMEM((n_blk, d_in, piece), F32),
            pltpu.VMEM((n_blk, d_in, piece), BF16),
            pltpu.VMEM((n_blk, d_in, piece), BF16),
            pltpu.VMEM((n_blk, wch + 8, hid), F32),
            pltpu.VMEM((n_blk, wch + 8, hid), F32),
            pltpu.VMEM((wch + 8, hid), F32),
            pltpu.VMEM((n_rep, wch + 8, hid), F32),
            pltpu.VMEM((wch, hid), F32),
            pltpu.VMEM((n_blk, wch, hid), F32),
            sem((n_blk,)), sem((n_blk,)),
            sem((n_rep,)), sem((n_rep,)),
            sem((n_rep,)), sem((n_rep,)),
            sem((n_blk,)), sem((n_blk,)),
            sem((n_blk,)), sem((n_blk,)),
            sem((n_rep,)), sem((n_rep,)),
            sem((n_blk,)), sem((n_blk,)),
            sem((7,)),
        ],
        compiler_params=pltpu.CompilerParams(
            collective_id=0, has_side_effects=True, vmem_limit_bytes=VMEM
        ),
    )(
        *[pltpu.with_memory_space_constraint(x, pltpu.HBM) for x in (
            features, edge_rows, edge_cols, weight, bias.reshape(1, hid),
            train_mask.reshape(panel // CB, CB), upstream,
        )]
    )
    act, gf, gw, gb = pl.pallas_call(
        write_out,
        out_shape=shapes,
        in_specs=[anywhere] * 4,
        out_specs=(hbm,) * 4,
        scratch_shapes=[sem((4,))],
        compiler_params=pltpu.CompilerParams(vmem_limit_bytes=VMEM),
    )(*results)
    return act, gf, gw, gb.reshape(hid)


def solution(mesh):
    n_blk, n_rep = mesh.shape["blk"], mesh.shape["rep"]
    return jax.shard_map(
        functools.partial(on_device, n_blk, n_rep),
        mesh=mesh,
        in_specs=(
            P(("blk", "rep"), None),
            P("blk", None, "rep", None),
            P("blk", None, "rep", None),
            P(),
            P(),
            P("blk", None),
            P("blk"),
        ),
        out_specs=(P(("blk", "rep"), None), P(("blk", "rep"), None), P(), P()),
        check_vma=False,
    )
```
